32 devices in a mesh: pts: 16 (over z, y, x), rep: 2 (over core).
Axes of the slice: x: 2, y: 2, z: 4, core: 2. Of those that a mesh axis runs over, the one named last changes fastest.
Arguments:
- src_points: bfloat16 [49152, 256], P('pts'), may hold values from -7 to 7
- tgt_points: bfloat16 [49152, 256], P('pts'), may hold values from -7 to 7
- pair_source: int32 [512], P(('pts', 'rep')), may hold values from -1 to 383, as said below
- pair_target: int32 [512], P(('pts', 'rep')), may hold values from -1 to 383, as said below
- pair_count: int32 [32], P(('pts', 'rep')), may hold values from 12 to 16, as said below
Outputs:
- source_dual: float32 [49152], P('pts')
- target_dual: float32 [49152], P('pts')
- target_grad: float32 [49152, 256], P('pts')
The draws below stay inside these ranges and needn't reach their ends.
Inputs may be any that keep to these rules, and one draw needn't show every extreme that they name: `pair_source`: for the device at index d of pts+rep (pts index p = d // 2, rep index r = d % 2), the first pair_count[d] of its 16 slots name source blocks p * 24 to (p + 1) * 24 - 1; its other slots hold -1. `pair_target`: A listed target block t has owner t // 24; one device's listed slots name different owners, and only blocks whose index t % 24 lies in r * 12 to (r + 1) * 12 - 1; unlisted slots hold -1. No pair of blocks is listed twice; every source block and every target block is listed somewhere; some owner is named by every device. `pair_count`: some device lists 16 pairs.
All inputs are finite; a program needn't handle non-finite values.
Results may differ from the reference program's by a relative error of at most 0.0016.
Values may be sent and summed in bfloat16 or wider, within the bound.
A program may use at most 192 MiB of HBM per device.

```python
import jax
import jax.numpy as jnp
from jax import lax

DIM = 256
BLOCK = 128
BLK_DEV = 24
TGT_MAX = 96
ITERS = 3
SLOTS_DEV = 16
BLOCKS = 384
POINTS = 49152
SLOTS = 512
N_PTS = 16
N_REP = 2


def point_cloud(key, salt):
    noise_key = jax.random.fold_in(jax.random.fold_in(key, salt), 0)
    point_rows = N_PTS * BLK_DEV * BLOCK
    return jnp.clip(jax.random.normal(noise_key, (point_rows, DIM), jnp.float32), -6.0, 6.0).astype(jnp.bfloat16)


def draw_src_points(key, part):
    return point_cloud(key, 3)


def draw_tgt_points(key, part):
    return point_cloud(key, 5)


def pair_tables(key):
    devices = N_PTS * N_REP
    half_blocks = BLK_DEV // N_REP
    most = min(TGT_MAX, N_PTS)
    spare = most - half_blocks - 1
    subkeys = [jax.random.fold_in(key, 100 + j) for j in range(8)]
    offsets = jax.random.permutation(subkeys[0], N_PTS)[:half_blocks]
    central = jax.random.randint(subkeys[1], (), 0, N_PTS)
    device_rank = jnp.arange(devices) // N_REP
    device_side = jnp.arange(devices) % N_REP
    fixed_owner = (device_rank[:, None] + offsets[None, :]) % N_PTS
    lanes = jnp.arange(N_PTS)
    taken = jnp.any(fixed_owner[:, :, None] == lanes[None, None, :], axis=1)
    central_fresh = jnp.logical_not(jnp.any(fixed_owner == central, axis=1))
    orders = jax.vmap(lambda sub: jax.random.permutation(sub, N_PTS))(jax.random.split(subkeys[2], devices))
    open_lane = jnp.logical_not(jnp.take_along_axis(taken, orders, axis=1)) & (orders != central)
    running = jnp.cumsum(open_lane.astype(jnp.int32), axis=1)
    first_draw = jax.random.randint(subkeys[3], (devices,), 0, spare + 1)
    second_draw = jax.random.randint(subkeys[4], (devices,), 0, spare + 1)
    wanted = first_draw * (2 * spare + second_draw) // (3 * spare)
    heavy = jax.random.randint(subkeys[5], (), 0, devices)
    wanted = jnp.where(jnp.arange(devices) == heavy, most - half_blocks - central_fresh.astype(jnp.int32), wanted)
    extra_live = open_lane & (running <= wanted[:, None])
    owners = jnp.concatenate([fixed_owner, jnp.full((devices, 1), central, jnp.int32), orders.astype(jnp.int32)], axis=1)
    live = jnp.concatenate([jnp.ones((devices, half_blocks), bool), central_fresh[:, None], extra_live], axis=1)
    span = half_blocks + 1 + N_PTS
    position = jnp.arange(span)[None, :]
    local_target = jnp.where(position < half_blocks, position, jax.random.randint(subkeys[6], (devices, span), 0, half_blocks))
    target_local = device_side[:, None] * half_blocks + local_target
    source_local = jnp.where(position < half_blocks, device_side[:, None] * half_blocks + position, jax.random.randint(subkeys[7], (devices, span), 0, BLK_DEV))
    ranking = jnp.argsort(jnp.where(live, 0, 1), axis=1, stable=True)[:, :most]
    listed_count = jnp.sum(live.astype(jnp.int32), axis=1)
    slot_live = jnp.arange(most)[None, :] < listed_count[:, None]
    owner_sel = jnp.take_along_axis(owners, ranking, axis=1)
    target_sel = jnp.take_along_axis(target_local, ranking, axis=1)
    source_sel = jnp.take_along_axis(source_local, ranking, axis=1)
    targets = jnp.where(slot_live, owner_sel * BLK_DEV + target_sel, -1).astype(jnp.int32)
    sources = jnp.where(slot_live, device_rank[:, None] * BLK_DEV + source_sel, -1).astype(jnp.int32)
    return (sources.reshape(-1), targets.reshape(-1), listed_count.astype(jnp.int32))


def draw_pair_source(key, part):
    return pair_tables(key)[0]


def draw_pair_target(key, part):
    return pair_tables(key)[1]


def draw_pair_count(key, part):
    return pair_tables(key)[2]


def setup_inputs(seed: int = 0) -> dict:
    splits = jax.random.split(jax.random.key(seed), 6)
    src_points = draw_src_points(jax.random.fold_in(splits[5], 71), 0)
    tgt_points = draw_tgt_points(jax.random.fold_in(splits[5], 71), 0)
    pair_source = draw_pair_source(jax.random.fold_in(splits[5], 71), 0)
    pair_target = draw_pair_target(jax.random.fold_in(splits[5], 71), 0)
    pair_count = draw_pair_count(jax.random.fold_in(splits[5], 71), 0)
    return {"src_points": src_points, "tgt_points": tgt_points, "pair_source": pair_source, "pair_target": pair_target, "pair_count": pair_count}


EPSILON = 0.05
NEG_BIG = -1.0e30


def pair_costs(source_rows, target_rows):
    xs = source_rows.astype(jnp.float32)
    ys = target_rows.astype(jnp.float32)
    inner_dot = jnp.einsum("gid,gjd->gij", xs, ys)
    source_sq = jnp.sum(xs * xs, axis=2)
    target_sq = jnp.sum(ys * ys, axis=2)
    return (source_sq[:, :, None] + target_sq[:, None, :] - 2.0 * inner_dot) / DIM


def settle(peaks, masses, block_key, listed):
    peaks = jnp.where(listed[:, None], peaks, NEG_BIG)
    masses = jnp.where(listed[:, None], masses, 0.0)
    maxima = jnp.full((BLOCKS, BLOCK), NEG_BIG, jnp.float32).at[block_key].max(peaks)
    totals = jnp.zeros((BLOCKS, BLOCK), jnp.float32).at[block_key].add(masses * jnp.exp(peaks - maxima[block_key]))
    return -EPSILON * (maxima + jnp.log(totals))


def reference(src_points, tgt_points, pair_source, pair_target, pair_count):
    source_blocks = src_points.reshape(BLOCKS, BLOCK, DIM)
    target_blocks = tgt_points.reshape(BLOCKS, BLOCK, DIM)
    slot_ids = jnp.arange(SLOTS, dtype=jnp.int32)
    listed = (slot_ids % SLOTS_DEV) < pair_count[slot_ids // SLOTS_DEV]
    source_ids = jnp.where(listed, pair_source, 0).astype(jnp.int32)
    target_ids = jnp.where(listed, pair_target, 0).astype(jnp.int32)
    groups = SLOTS // SLOTS_DEV
    source_groups = source_ids.reshape(groups, SLOTS_DEV)
    target_groups = target_ids.reshape(groups, SLOTS_DEV)
    listed_groups = listed.reshape(groups, SLOTS_DEV)

    def costs_of(group_no):
        return pair_costs(source_blocks[source_groups[group_no]], target_blocks[target_groups[group_no]])

    def row_update(target_dual):
        def one_group(group_no):
            scores = (target_dual[target_groups[group_no]][:, None, :] - costs_of(group_no)) / EPSILON
            peaks = jnp.max(scores, axis=2)
            return peaks, jnp.sum(jnp.exp(scores - peaks[:, :, None]), axis=2)

        peaks, masses = lax.map(one_group, jnp.arange(groups))
        return settle(peaks.reshape(SLOTS, BLOCK), masses.reshape(SLOTS, BLOCK), source_ids, listed)

    def column_update(source_dual):
        def one_group(group_no):
            scores = (source_dual[source_groups[group_no]][:, :, None] - costs_of(group_no)) / EPSILON
            peaks = jnp.max(scores, axis=1)
            return peaks, jnp.sum(jnp.exp(scores - peaks[:, None, :]), axis=1)

        peaks, masses = lax.map(one_group, jnp.arange(groups))
        return settle(peaks.reshape(SLOTS, BLOCK), masses.reshape(SLOTS, BLOCK), target_ids, listed)

    target_dual = jnp.zeros((BLOCKS, BLOCK), jnp.float32)
    source_dual = jnp.zeros((BLOCKS, BLOCK), jnp.float32)
    for round_no in range(ITERS):
        source_dual = row_update(target_dual)
        target_dual = column_update(source_dual)

    def gradient_step(carry, group_no):
        numerator, column_mass = carry
        plan = jnp.exp((source_dual[source_groups[group_no]][:, :, None] + target_dual[target_groups[group_no]][:, None, :] - costs_of(group_no)) / EPSILON)
        plan = jnp.where(listed_groups[group_no][:, None, None], plan, 0.0)
        weights = lax.optimization_barrier(plan.astype(jnp.bfloat16)).astype(jnp.float32)
        partial_value = jnp.einsum("gij,gid->gjd", weights, source_blocks[source_groups[group_no]].astype(jnp.float32))
        numerator = numerator.at[target_groups[group_no]].add(partial_value)
        column_mass = column_mass.at[target_groups[group_no]].add(jnp.sum(plan, axis=1))
        return (numerator, column_mass), None

    start = (jnp.zeros((BLOCKS, BLOCK, DIM), jnp.float32), jnp.zeros((BLOCKS, BLOCK), jnp.float32))
    (numerator, column_mass), unused = lax.scan(gradient_step, start, jnp.arange(groups))
    target_grad = target_blocks.astype(jnp.float32) * column_mass[:, :, None] - numerator
    return source_dual.reshape(POINTS), target_dual.reshape(POINTS), target_grad.reshape(POINTS, DIM)
```

```python
import functools

import jax
import jax.numpy as jnp
from jax import lax
from jax.experimental import pallas as pl
from jax.experimental.pallas import tpu as pltpu
from jax.sharding import PartitionSpec as P

BLOCK = 128
ITERS = 3
EPSILON = 0.05
NEG_BIG = -1e30
MESH = pl.DeviceIdType.MESH
VMEM_BYTES = 56 * 1024 * 1024


def loop(lower, upper, body):
    def step(i, carry):
        body(i)
        return carry

    lax.fori_loop(lower, upper, step, 0)


def grouped(total, size, body):
    def step(i):
        for k in range(size):
            body(i * size + k)

    loop(0, total // size, step)


def flipped(me, d, n):
    if n & (n - 1):
        return lax.rem(me + d, n)
    out, bit = 0, 1
    while bit < n:
        out = out + bit * (((me // bit) + (d // bit)) % 2)
        bit *= 2
    return out


def as_column(row):
    return jnp.transpose(jnp.broadcast_to(row, (BLOCK, BLOCK)))


def square_row(block):
    values = block.astype(jnp.float32)
    column = jnp.sum(values * values, axis=1, keepdims=True)
    return jnp.transpose(jnp.broadcast_to(column, (BLOCK, BLOCK)))[0:1, :]


def combine(peaks, masses, keys, key):
    member = keys == key
    top = jnp.max(jnp.where(member, peaks, NEG_BIG), axis=0, keepdims=True)
    parts = masses * jnp.exp(jnp.where(member, peaks - top, NEG_BIG))
    return top, jnp.sum(jnp.where(member, parts, 0.0), axis=0, keepdims=True)


def exchange_kernel(
    n, blocks, half, scale,
    source_pick, source_keys, want_rows, src_hbm, tgt_hbm,
    rx_out, ids_out, a_out, b_out, source_out, target_out,
    src, tgt, out_x, rx, score, score_t, b_col, ids_in, ids_all, ids_smem, id_keys,
    stats_out, stats_in, peak_rows, mass_rows, rep_out, rep_in, a_src, a_send, a_in, a_all, b_all,
    x_sq, y_sq,
    load_sem, x_send, x_recv, id_send, id_recv, fwd_send, fwd_recv, keep_sem,
    stat_send, stat_recv, a_ssem, a_rsem, rep_send, rep_recv, tail_send, tail_recv,
):
    me = lax.axis_index("pts")
    side = lax.axis_index("rep")
    other = 1 - side
    first = side * half

    load_src = pltpu.make_async_copy(src_hbm, src, load_sem.at[0])
    load_tgt = pltpu.make_async_copy(tgt_hbm, tgt, load_sem.at[1])
    load_src.start()
    load_tgt.start()

    barrier = pltpu.get_barrier_semaphore()

    def greet(d):
        pl.semaphore_signal(
            barrier, inc=1, device_id=(lax.rem(me + d, n), side), device_id_type=MESH
        )

    loop(1, n, greet)
    pl.semaphore_signal(barrier, inc=1, device_id=(me, other), device_id_type=MESH)
    pl.semaphore_wait(barrier, n)

    def to_peer(src_ref, dst_ref, send_sem, recv_sem, peer):
        return pltpu.make_async_remote_copy(
            src_ref=src_ref, dst_ref=dst_ref, send_sem=send_sem, recv_sem=recv_sem,
            device_id=(peer, side), device_id_type=MESH,
        )

    def to_twin(src_ref, dst_ref, send_sem, recv_sem):
        return pltpu.make_async_remote_copy(
            src_ref=src_ref, dst_ref=dst_ref, send_sem=send_sem, recv_sem=recv_sem,
            device_id=(me, other), device_id_type=MESH,
        )

    def id_copy(peer, slot):
        return to_peer(want_rows.at[peer], ids_in.at[slot], id_send.at[peer], id_recv.at[slot], peer)

    def x_copy(peer, slot):
        return to_peer(out_x.at[peer], rx.at[slot], x_send.at[peer], x_recv.at[slot], peer)

    def stat_copy(it, peer, slot):
        return to_peer(
            stats_out.at[it, peer], stats_in.at[it, slot],
            stat_send.at[it, peer], stat_recv.at[it, slot], peer,
        )

    def a_copy(it, peer, slot):
        return to_peer(
            a_send.at[it, peer], a_in.at[it, slot], a_ssem.at[it, peer], a_rsem.at[it, slot], peer
        )

    def keep_copy(slot):
        return pltpu.make_async_copy(rx.at[slot], rx_out.at[side, slot], keep_sem.at[slot])

    def forward_copy(slot, which):
        return to_twin(
            rx.at[slot], rx_out.at[which, slot], fwd_send.at[slot], fwd_recv.at[slot]
        )

    loop(1, n, lambda d: id_copy(lax.rem(me + d, n), me).start())
    load_src.wait()

    def send_block(d):
        peer = flipped(me, d, n)
        out_x[peer] = src[jnp.maximum(source_pick[peer], 0)]
        x_copy(peer, me).start()

    loop(n // 2, n, send_block)
    loop(1, n // 2, send_block)
    rx[me] = src[jnp.maximum(source_pick[me], 0)]
    ids_in[me] = want_rows[me]
    load_tgt.wait()

    def source_squares(b):
        x_sq[pl.ds(b, 1), :] = scale * square_row(src[b])

    def target_squares(b):
        row = scale * square_row(tgt[b])
        y_sq[b // half, pl.ds(b % half, 1), :] = row
        b_col[b] = as_column(-row)

    loop(0, blocks, source_squares)
    loop(0, blocks, target_squares)

    def take_id(d):
        peer = lax.rem(me + d, n)
        id_copy(peer, peer).wait_recv()

    loop(1, n, take_id)
    ids_move = pltpu.make_async_copy(ids_in, ids_smem, load_sem.at[2])
    ids_move.start()

    def id_row(q):
        row = ids_in[q]
        id_keys[pl.ds(q, 1), :] = row
        ids_all[side, pl.ds(q, 1), :] = row

    loop(0, n, id_row)
    ids_move.wait()

    def row_stats(it, q, local_target):
        terms = b_col[local_target] + score_t[q]
        top = jnp.max(terms, axis=0, keepdims=True)
        stats_out[it, q, 0:1, :] = top
        stats_out[it, q, 1:2, :] = jnp.sum(jnp.exp(terms - top), axis=0, keepdims=True)

    def local_id(q):
        return jnp.maximum(ids_smem[q, 0, 0], 0)

    def first_visit(q):
        keep_copy(q).start()
        forward_copy(q, side).start()
        pick = local_id(q)
        grid = lax.dot_general(
            rx[q], tgt[pick], (((1,), (1,)), ((), ())), preferred_element_type=jnp.float32
        ) * (2.0 * scale)
        grid_t = jnp.transpose(grid)
        score[q] = grid
        score_t[q] = grid_t
        terms = b_col[pick] + grid_t
        top = jnp.max(terms, axis=0, keepdims=True)
        stats_out[0, q, 0:1, :] = top
        stats_out[0, q, 1:2, :] = jnp.sum(jnp.exp(terms - top), axis=0, keepdims=True)

    def own_stats(it):
        stats_in[it, me] = stats_out[it, me]

    first_visit(me)
    own_stats(0)

    def arrival(d):
        peer = flipped(me, d, n)
        x_copy(peer, peer).wait_recv()
        first_visit(peer)
        stat_copy(0, peer, me).start()

    loop(n // 2, n, arrival)
    loop(1, n // 2, arrival)

    for it in range(ITERS):
        def take_stats(d):
            peer = lax.rem(me + d, n)
            stat_copy(it, peer, peer).wait_recv()

        loop(1, n, take_stats)

        def stat_row(p):
            peak_rows[pl.ds(p, 1), :] = stats_in[it, p, 0:1, :]
            mass_rows[pl.ds(p, 1), :] = stats_in[it, p, 1:2, :]

        grouped(n, 8, stat_row)
        peaks, masses, keys = peak_rows[...], mass_rows[...], source_keys[...]
        for b in range(blocks):
            top, total = combine(peaks, masses, keys, b)
            rep_out[it, 0, b:b + 1, :] = top
            rep_out[it, 1, b:b + 1, :] = total
        swap = to_twin(rep_out.at[it], rep_in.at[it], rep_send.at[it], rep_recv.at[it])
        swap.start()
        swap.wait_recv()
        top = jnp.maximum(rep_out[it, 0], rep_in[it, 0])
        total = rep_out[it, 1] * jnp.exp(rep_out[it, 0] - top) + rep_in[it, 1] * jnp.exp(
            rep_in[it, 0] - top
        )
        a_src[...] = -(top + jnp.log(total))

        def send_a(d):
            peer = lax.rem(me + d, n)
            a_send[it, peer] = a_src[pl.ds(jnp.maximum(source_pick[peer], 0), 1), :]
            a_copy(it, peer, me).start()

        loop(1, n, send_a)
        a_in[it, me] = a_src[pl.ds(jnp.maximum(source_pick[me], 0), 1), :]

        def take_a(d):
            peer = lax.rem(me + d, n)
            a_copy(it, peer, peer).wait_recv()

        loop(1, n, take_a)

        def column_visit(q):
            terms = as_column(a_in[it, q]) + score[q]
            top = jnp.max(terms, axis=0, keepdims=True)
            peak_rows[pl.ds(q, 1), :] = top
            mass_rows[pl.ds(q, 1), :] = jnp.sum(jnp.exp(terms - top), axis=0, keepdims=True)

        grouped(n, 4, column_visit)
        peaks, masses, keys = peak_rows[...], mass_rows[...], id_keys[...]
        for b in range(half):
            top, total = combine(peaks, masses, keys, b + first)
            row = -(top + jnp.log(total))
            if it + 1 < ITERS:
                b_col[first + b] = as_column(row)
            else:
                b_all[side, b:b + 1, :] = row

        if it + 1 < ITERS:
            grouped(n, 4, lambda q: row_stats(it + 1, q, local_id(q)))
            own_stats(it + 1)

            def send_stats(d):
                stat_copy(it + 1, lax.rem(me + d, n), me).start()

            loop(1, n, send_stats)

    def last_row(q):
        a_all[side, pl.ds(q, 1), :] = a_in[ITERS - 1, q]

    grouped(n, 8, last_row)
    tails = [
        to_twin(ref.at[side], ref.at[side], tail_send.at[k], tail_recv.at[k])
        for k, ref in enumerate((ids_all, a_all, b_all))
    ]
    for copy in tails:
        copy.start()
    source_out[...] = EPSILON * (a_src[...] + x_sq[...])

    def finish_local(q):
        keep_copy(q).wait()
        forward_copy(q, other).wait_recv()
        forward_copy(q, side).wait_send()

    loop(0, n, finish_local)

    def finish_sends(d):
        peer = lax.rem(me + d, n)
        id_copy(peer, me).wait_send()
        x_copy(peer, me).wait_send()
        for it in range(ITERS):
            stat_copy(it, peer, me).wait_send()
            a_copy(it, peer, me).wait_send()

    loop(1, n, finish_sends)
    for it in range(ITERS):
        to_twin(rep_out.at[it], rep_in.at[it], rep_send.at[it], rep_recv.at[it]).wait_send()
    for k, ref in enumerate((ids_all, a_all, b_all)):
        to_twin(ref.at[other], ref.at[other], tail_send.at[k], tail_recv.at[k]).wait_recv()
        tails[k].wait_send()
    ids_out[...] = ids_all[...]
    a_out[...] = a_all[...]
    b_out[...] = b_all[...]
    target_out[...] = EPSILON * (b_all[...] + y_sq[...])


def gradient_kernel(pairs, blocks, scale, ids, rx, a_rows, b_rows, tgt, grad, b_col, mass):
    def prepare(b):
        grad[b] = jnp.zeros(grad.shape[1:], jnp.float32)
        mass[b] = jnp.zeros((BLOCK, BLOCK), jnp.float32)
        b_col[b] = as_column(b_rows[pl.ds(b, 1), :])

    grouped(blocks, 4, prepare)

    def visit(k0):
        results = []
        for k in range(4):
            q = k0 * 4 + k
            target = ids[q, 0]
            pick = jnp.maximum(target, 0)
            grid = lax.dot_general(
                tgt[pick], rx[q], (((1,), (1,)), ((), ())), preferred_element_type=jnp.float32
            ) * (2.0 * scale)
            plan = jnp.exp(b_col[pick] + (grid + a_rows[pl.ds(q, 1), :]))
            plan = jnp.where(target >= 0, plan, 0.0)
            part = jnp.dot(plan.astype(jnp.bfloat16), rx[q], preferred_element_type=jnp.float32)
            results.append((pick, plan, part))
        for pick, plan, part in results:
            grad[pick] += part
            mass[pick] += plan

    loop(0, pairs // 4, visit)

    def finish(b):
        column = jnp.sum(mass[b], axis=1, keepdims=True)
        grad[b] = tgt[b].astype(jnp.float32) * column - grad[b]

    grouped(blocks, 2, finish)


def on_device(src_points, tgt_points, pair_source, pair_target, pair_count):
    n = lax.axis_size("pts")
    reps = lax.axis_size("rep")
    rows, dim = src_points.shape
    blocks = rows // BLOCK
    half = blocks // reps
    scale = 1.0 / EPSILON / dim
    src = src_points.reshape(blocks, BLOCK, dim)
    tgt = tgt_points.reshape(blocks, BLOCK, dim)
    usable = jnp.arange(pair_source.shape[0]) < pair_count[0]
    owner = pair_target // blocks
    matched = (owner[:, None] == jnp.arange(n)[None, :]) & usable[:, None]
    wanted = jnp.max(jnp.where(matched, (pair_target % blocks)[:, None], -1), axis=0)
    picked = jnp.max(jnp.where(matched, (pair_source % blocks)[:, None], -1), axis=0)
    source_keys = jnp.broadcast_to(picked[:, None], (n, BLOCK))
    want_rows = jnp.broadcast_to(wanted[:, None, None], (n, 1, BLOCK))

    f32, bf16, i32 = jnp.float32, jnp.bfloat16, jnp.int32
    shape = jax.ShapeDtypeStruct
    vmem = pl.BlockSpec(memory_space=pltpu.VMEM)
    smem = pl.BlockSpec(memory_space=pltpu.SMEM)
    hbm = pl.BlockSpec(memory_space=pl.ANY)
    dma = pltpu.SemaphoreType.DMA
    with jax.named_scope("exchange_and_sweeps"):
        rx, ids, a_rows, b_rows, source_dual, target_dual = pl.pallas_call(
            functools.partial(exchange_kernel, n, blocks, half, scale),
            out_shape=(
                shape((reps, n, BLOCK, dim), bf16),
                shape((reps, n, BLOCK), i32),
                shape((reps, n, BLOCK), f32),
                shape((reps, half, BLOCK), f32),
                shape((blocks, BLOCK), f32),
                shape((reps, half, BLOCK), f32),
            ),
            in_specs=[smem, vmem, vmem, hbm, hbm],
            out_specs=(hbm, vmem, vmem, vmem, vmem, vmem),
            scratch_shapes=[
                pltpu.VMEM((blocks, BLOCK, dim), bf16),
                pltpu.VMEM((blocks, BLOCK, dim), bf16),
                pltpu.VMEM((n, BLOCK, dim), bf16),
                pltpu.VMEM((n, BLOCK, dim), bf16),
                pltpu.VMEM((n, BLOCK, BLOCK), f32),
                pltpu.VMEM((n, BLOCK, BLOCK), f32),
                pltpu.VMEM((blocks, BLOCK, BLOCK), f32),
                pltpu.VMEM((n, 1, BLOCK), i32),
                pltpu.VMEM((reps, n, BLOCK), i32),
                pltpu.SMEM((n, 1, BLOCK), i32),
                pltpu.VMEM((n, BLOCK), i32),
                pltpu.VMEM((ITERS, n, 2, BLOCK), f32),
                pltpu.VMEM((ITERS, n, 2, BLOCK), f32),
                pltpu.VMEM((n, BLOCK), f32),
                pltpu.VMEM((n, BLOCK), f32),
                pltpu.VMEM((ITERS, 2, blocks, BLOCK), f32),
                pltpu.VMEM((ITERS, 2, blocks, BLOCK), f32),
                pltpu.VMEM((blocks, BLOCK), f32),
                pltpu.VMEM((ITERS, n, 1, BLOCK), f32),
                pltpu.VMEM((ITERS, n, 1, BLOCK), f32),
                pltpu.VMEM((reps, n, BLOCK), f32),
                pltpu.VMEM((reps, half, BLOCK), f32),
                pltpu.VMEM((blocks, BLOCK), f32),
                pltpu.VMEM((reps, half, BLOCK), f32),
                dma((3,)),
                dma((n,)), dma((n,)), dma((n,)), dma((n,)), dma((n,)), dma((n,)), dma((n,)),
                dma((ITERS, n)), dma((ITERS, n)), dma((ITERS, n)), dma((ITERS, n)),
                dma((ITERS,)), dma((ITERS,)), dma((3,)), dma((3,)),
            ],
            compiler_params=pltpu.CompilerParams(
                collective_id=0, has_side_effects=True, vmem_limit_bytes=VMEM_BYTES
            ),
            name="exchange_and_sweeps",
        )(picked, source_keys, want_rows, src, tgt)
    pairs = reps * n
    with jax.named_scope("gradient"):
        grad = pl.pallas_call(
            functools.partial(gradient_kernel, pairs, blocks, scale),
            out_shape=shape((blocks, BLOCK, dim), f32),
            in_specs=[smem, vmem, vmem, vmem, vmem],
            out_specs=vmem,
            scratch_shapes=[
                pltpu.VMEM((blocks, BLOCK, BLOCK), f32),
                pltpu.VMEM((blocks, BLOCK, BLOCK), f32),
            ],
            compiler_params=pltpu.CompilerParams(vmem_limit_bytes=VMEM_BYTES),
            name="gradient",
        )(
            ids.reshape(pairs, BLOCK),
            rx.reshape(pairs, BLOCK, dim),
            a_rows.reshape(pairs, BLOCK),
            b_rows.reshape(blocks, BLOCK),
            tgt,
        )
    return source_dual.reshape(-1), target_dual.reshape(-1), grad.reshape(rows, dim)


def solution(mesh):
    return jax.shard_map(
        on_device,
        mesh=mesh,
        in_specs=(
            P("pts", None),
            P("pts", None),
            P(("pts", "rep")),
            P(("pts", "rep")),
            P(("pts", "rep")),
        ),
        out_specs=(P("pts"), P("pts"), P("pts", None)),
        check_vma=False,
    )
```

```python
import functools

import jax
import jax.numpy as jnp
from jax import lax
from jax.experimental import pallas as pl
from jax.experimental.pallas import tpu as pltpu
from jax.sharding import PartitionSpec as P

BLOCK = 128
ITERS = 3
EPSILON = 0.05
NEG_BIG = -1e30
MESH = pl.DeviceIdType.MESH
VMEM_BYTES = 56 * 1024 * 1024


def loop(lower, upper, body):
    def step(i, carry):
        body(i)
        return carry

    lax.fori_loop(lower, upper, step, 0)


def grouped(total, size, body):
    def step(i):
        for k in range(size):
            body(i * size + k)

    loop(0, total // size, step)


def flipped(me, d, n):
    if n & (n - 1):
        return lax.rem(me + d, n)
    out, bit = 0, 1
    while bit < n:
        out = out + bit * (((me // bit) + (d // bit)) % 2)
        bit *= 2
    return out


def as_column(row):
    return jnp.transpose(jnp.broadcast_to(row, (BLOCK, BLOCK)))


def columns_of(rows):
    turned = jnp.transpose(rows)
    return [jnp.broadcast_to(turned[:, k:k + 1], (BLOCK, BLOCK)) for k in range(rows.shape[0])]


def square_row(block):
    values = block.astype(jnp.float32)
    column = jnp.sum(values * values, axis=1, keepdims=True)
    return jnp.transpose(jnp.broadcast_to(column, (BLOCK, BLOCK)))[0:1, :]


def combine(peaks, masses, keys, key):
    member = keys == key
    top = jnp.max(jnp.where(member, peaks, NEG_BIG), axis=0, keepdims=True)
    parts = masses * jnp.exp(jnp.where(member, peaks - top, NEG_BIG))
    return top, jnp.sum(jnp.where(member, parts, 0.0), axis=0, keepdims=True)


def exchange_kernel(
    n, blocks, half, scale,
    source_pick, wanted, src_hbm, tgt_hbm,
    rx_out, ids_out, a_out, b_out, source_out, target_out,
    src, tgt, out_x, rx, score, score_t, b_col, want_rows, ids_in, ids_all, ids_smem, id_keys,
    key_all, stats_out, stats_in, peak_rows, mass_rows, a_src, a_send, a_in, a_rows, a_all, b_all,
    b_pad, x_sq, y_sq,
    load_sem, x_send, x_recv, id_send, id_recv, fwd_send, fwd_recv, keep_sem,
    stat_send, stat_recv, a_ssem, a_rsem, tail_send, tail_recv,
):
    me = lax.axis_index("pts")
    side = lax.axis_index("rep")
    other = 1 - side
    first = side * half

    load_src = pltpu.make_async_copy(src_hbm, src, load_sem.at[0])
    load_tgt = pltpu.make_async_copy(tgt_hbm, tgt, load_sem.at[1])
    load_src.start()
    load_tgt.start()

    barrier = pltpu.get_barrier_semaphore()

    def greet(d):
        pl.semaphore_signal(
            barrier, inc=1, device_id=(lax.rem(me + d, n), side), device_id_type=MESH
        )

    def greet_other(d):
        pl.semaphore_signal(
            barrier, inc=1, device_id=(lax.rem(me + d, n), other), device_id_type=MESH
        )

    loop(1, n, greet)
    loop(0, n, greet_other)

    def list_row(p):
        want_rows[p] = jnp.full((1, BLOCK), wanted[p], jnp.int32)
        key_all[side, pl.ds(p, 1), :] = jnp.full((1, BLOCK), source_pick[p], jnp.int32)

    grouped(n, 8, list_row)
    pl.semaphore_wait(barrier, 2 * n - 1)

    def to_peer(src_ref, dst_ref, send_sem, recv_sem, peer):
        return pltpu.make_async_remote_copy(
            src_ref=src_ref, dst_ref=dst_ref, send_sem=send_sem, recv_sem=recv_sem,
            device_id=(peer, side), device_id_type=MESH,
        )

    def to_twin(src_ref, dst_ref, send_sem, recv_sem):
        return pltpu.make_async_remote_copy(
            src_ref=src_ref, dst_ref=dst_ref, send_sem=send_sem, recv_sem=recv_sem,
            device_id=(me, other), device_id_type=MESH,
        )

    def id_copy(peer, slot):
        return to_peer(want_rows.at[peer], ids_in.at[slot], id_send.at[peer], id_recv.at[slot], peer)

    def x_copy(peer, slot):
        return to_peer(out_x.at[peer], rx.at[slot], x_send.at[peer], x_recv.at[slot], peer)

    def stat_copy(it, peer, to_side, from_side, slot):
        return pltpu.make_async_remote_copy(
            src_ref=stats_out.at[it, peer], dst_ref=stats_in.at[it, from_side, slot],
            send_sem=stat_send.at[it, to_side, peer], recv_sem=stat_recv.at[it, from_side, slot],
            device_id=(peer, to_side), device_id_type=MESH,
        )

    def a_copy(it, peer, slot):
        return to_peer(
            a_send.at[it, peer], a_in.at[it, slot], a_ssem.at[it, peer], a_rsem.at[it, slot], peer
        )

    def keep_copy(slot):
        return pltpu.make_async_copy(rx.at[slot], rx_out.at[side, slot], keep_sem.at[slot])

    def forward_copy(slot, which):
        return to_twin(
            rx.at[slot], rx_out.at[which, slot], fwd_send.at[slot], fwd_recv.at[slot]
        )

    def tail_copy(k, ref, which):
        return to_twin(ref.at[which], ref.at[which], tail_send.at[k], tail_recv.at[k])

    loop(1, n, lambda d: id_copy(lax.rem(me + d, n), me).start())
    tail_copy(3, key_all, side).start()
    load_src.wait()

    def send_block(d):
        peer = flipped(me, d, n)
        out_x[peer] = src[jnp.maximum(source_pick[peer], 0)]
        x_copy(peer, me).start()

    loop(n // 2, n, send_block)
    loop(1, n // 2, send_block)
    rx[me] = src[jnp.maximum(source_pick[me], 0)]
    ids_in[me] = want_rows[me]
    load_tgt.wait()
    b_pad[...] = jnp.zeros(b_pad.shape, jnp.float32)

    def source_squares(b):
        x_sq[pl.ds(b, 1), :] = scale * square_row(src[b])

    def target_squares(b):
        row = scale * square_row(tgt[b])
        y_sq[pl.ds(b, 1), :] = row
        b_col[b] = as_column(-row)

    loop(0, blocks, source_squares)
    loop(0, blocks, target_squares)

    def take_id(d):
        peer = lax.rem(me + d, n)
        id_copy(peer, peer).wait_recv()

    loop(1, n, take_id)
    ids_move = pltpu.make_async_copy(ids_in, ids_smem, load_sem.at[2])
    ids_move.start()

    def id_row(q):
        row = ids_in[q]
        id_keys[pl.ds(q, 1), :] = row
        ids_all[side, pl.ds(q, 1), :] = row

    loop(0, n, id_row)
    tail_copy(0, ids_all, side).start()
    ids_move.wait()

    def row_stats(it, q, local_target):
        terms = b_col[local_target] + score_t[q]
        top = jnp.max(terms, axis=0, keepdims=True)
        stats_out[it, q, 0:1, :] = top
        stats_out[it, q, 1:2, :] = jnp.sum(jnp.exp(terms - top), axis=0, keepdims=True)

    def local_id(q):
        return jnp.maximum(ids_smem[q, 0, 0], 0)

    def first_visit(q):
        keep_copy(q).start()
        forward_copy(q, side).start()
        pick = local_id(q)
        grid = lax.dot_general(
            rx[q], tgt[pick], (((1,), (1,)), ((), ())), preferred_element_type=jnp.float32
        ) * (2.0 * scale)
        grid_t = jnp.transpose(grid)
        score[q] = grid
        score_t[q] = grid_t
        terms = b_col[pick] + grid_t
        top = jnp.max(terms, axis=0, keepdims=True)
        stats_out[0, q, 0:1, :] = top
        stats_out[0, q, 1:2, :] = jnp.sum(jnp.exp(terms - top), axis=0, keepdims=True)

    def own_stats(it):
        stats_in[it, side, me] = stats_out[it, me]

    first_visit(me)
    own_stats(0)
    stat_copy(0, me, other, side, me).start()

    def arrival(d):
        peer = flipped(me, d, n)
        x_copy(peer, peer).wait_recv()
        first_visit(peer)
        stat_copy(0, peer, other, side, me).start()
        stat_copy(0, peer, side, side, me).start()

    loop(n // 2, n, arrival)
    loop(1, n // 2, arrival)
    tail_copy(3, key_all, other).wait_recv()

    for it in range(ITERS):
        def take_stats(d):
            peer = lax.rem(me + d, n)
            stat_copy(it, peer, side, other, peer).wait_recv()
            stat_copy(it, peer, side, side, peer).wait_recv()

        stat_copy(it, me, side, other, me).wait_recv()
        loop(1, n, take_stats)
        for part in range(2):
            def stat_row(p):
                peak_rows[part, pl.ds(p, 1), :] = stats_in[it, part, p, 0:1, :]
                mass_rows[part, pl.ds(p, 1), :] = stats_in[it, part, p, 1:2, :]

            grouped(n, 8, stat_row)
        peaks = peak_rows[...].reshape(2 * n, BLOCK)
        masses = mass_rows[...].reshape(2 * n, BLOCK)
        keys = key_all[...].reshape(2 * n, BLOCK)
        for b in range(blocks):
            top, total = combine(peaks, masses, keys, b)
            a_src[b:b + 1, :] = -(top + jnp.log(total))

        def send_a(d):
            peer = lax.rem(me + d, n)
            a_send[it, peer] = a_src[pl.ds(jnp.maximum(source_pick[peer], 0), 1), :]
            a_copy(it, peer, me).start()

        loop(1, n, send_a)
        a_in[it, me] = a_src[pl.ds(jnp.maximum(source_pick[me], 0), 1), :]

        def take_a(d):
            peer = lax.rem(me + d, n)
            a_copy(it, peer, peer).wait_recv()

        loop(1, n, take_a)

        def a_row(q):
            a_rows[pl.ds(q, 1), :] = a_in[it, q]

        grouped(n, 8, a_row)
        if it + 1 == ITERS:
            a_all[side] = a_rows[...]
            tail_copy(1, a_all, side).start()

        def column_visits(chunk):
            base = chunk * 16
            for k, column in enumerate(columns_of(a_rows[pl.ds(pl.multiple_of(base, 16), 16), :])):
                terms = column + score[base + k]
                top = jnp.max(terms, axis=0, keepdims=True)
                peak_rows[0, pl.ds(base + k, 1), :] = top
                mass_rows[0, pl.ds(base + k, 1), :] = jnp.sum(
                    jnp.exp(terms - top), axis=0, keepdims=True
                )

        loop(0, n // 16, column_visits)
        peaks, masses, keys = peak_rows[0], mass_rows[0], id_keys[...]
        for b in range(half):
            top, total = combine(peaks, masses, keys, b + first)
            b_pad[b:b + 1, :] = -(top + jnp.log(total))
        if it + 1 == ITERS:
            b_all[side] = b_pad[0:half, :]
        else:
            for b, column in enumerate(columns_of(b_pad[...])[:half]):
                b_col[first + b] = column

            def next_rows(group):
                for k in range(4):
                    q = lax.rem(me + group * 4 + k, n)
                    row_stats(it + 1, q, local_id(q))
                for k in range(4):
                    d = group * 4 + k
                    q = lax.rem(me + d, n)
                    stat_copy(it + 1, q, other, side, me).start()

                    @pl.when(d > 0)
                    def _():
                        stat_copy(it + 1, q, side, side, me).start()

            loop(0, n // 4, next_rows)
            own_stats(it + 1)

    tail_copy(2, b_all, side).start()
    source_out[...] = EPSILON * (a_src[...] + x_sq[...])

    def finish_local(q):
        keep_copy(q).wait()
        forward_copy(q, other).wait_recv()
        forward_copy(q, side).wait_send()

    loop(0, n, finish_local)

    def finish_sends(d):
        peer = lax.rem(me + d, n)
        id_copy(peer, me).wait_send()
        x_copy(peer, me).wait_send()
        for it in range(ITERS):
            stat_copy(it, peer, other, side, me).wait_send()
            stat_copy(it, peer, side, side, me).wait_send()
            a_copy(it, peer, me).wait_send()

    loop(1, n, finish_sends)
    for it in range(ITERS):
        stat_copy(it, me, other, side, me).wait_send()
    tail_copy(3, key_all, side).wait_send()
    for k, ref in enumerate((ids_all, a_all, b_all)):
        tail_copy(k, ref, other).wait_recv()
        tail_copy(k, ref, side).wait_send()
    ids_out[...] = ids_all[...]
    a_out[...] = a_all[...]
    for part in range(2):
        b_out[part * half:(part + 1) * half, :] = b_all[part]
    target_out[...] = EPSILON * (b_out[...] + y_sq[...])


def gradient_kernel(
    pairs, blocks, scale, ids, rx_hbm, a_rows, b_rows, tgt, out, rx, grad, b_col, mass, sems, out_sems
):
    groups = pairs // 4

    def fetch(group):
        part = pl.ds(group * 4, 4)
        return pltpu.make_async_copy(rx_hbm.at[part], rx.at[part], sems.at[group])

    def store(b):
        return pltpu.make_async_copy(grad.at[b], out.at[b], out_sems.at[b])

    loop(0, groups, lambda group: fetch(group).start())
    for b, column in enumerate(columns_of(b_rows[...])):
        b_col[b] = column

    def prepare(b):
        grad[b] = jnp.zeros(grad.shape[1:], jnp.float32)
        mass[b] = jnp.zeros((BLOCK, BLOCK), jnp.float32)

    grouped(blocks, 4, prepare)

    def visit(group):
        fetch(group).wait()
        results = []
        for k in range(4):
            q = group * 4 + k
            target = ids[q, 0]
            pick = jnp.maximum(target, 0)
            grid = lax.dot_general(
                tgt[pick], rx[q], (((1,), (1,)), ((), ())), preferred_element_type=jnp.float32
            ) * (2.0 * scale)
            plan = jnp.exp(b_col[pick] + (grid + a_rows[pl.ds(q, 1), :]))
            plan = jnp.where(target >= 0, plan, 0.0)
            part = jnp.dot(plan.astype(jnp.bfloat16), rx[q], preferred_element_type=jnp.float32)
            results.append((pick, plan, part))
        for pick, plan, part in results:
            grad[pick] += part
            mass[pick] += plan

    loop(0, groups, visit)

    def finish(group):
        for k in range(4):
            b = group * 4 + k
            column = jnp.sum(mass[b], axis=1, keepdims=True)
            grad[b] = tgt[b].astype(jnp.float32) * column - grad[b]
        for k in range(4):
            store(group * 4 + k).start()

    loop(0, blocks // 4, finish)
    loop(0, blocks, lambda b: store(b).wait())


def on_device(src_points, tgt_points, pair_source, pair_target, pair_count):
    n = lax.axis_size("pts")
    reps = lax.axis_size("rep")
    rows, dim = src_points.shape
    blocks = rows // BLOCK
    half = blocks // reps
    scale = 1.0 / EPSILON / dim
    src = src_points.reshape(blocks, BLOCK, dim)
    tgt = tgt_points.reshape(blocks, BLOCK, dim)
    usable = jnp.arange(pair_source.shape[0]) < pair_count[0]
    owner = pair_target // blocks
    matched = (owner[:, None] == jnp.arange(n)[None, :]) & usable[:, None]
    wanted = jnp.max(jnp.where(matched, (pair_target % blocks)[:, None], -1), axis=0)
    picked = jnp.max(jnp.where(matched, (pair_source % blocks)[:, None], -1), axis=0)

    f32, bf16, i32 = jnp.float32, jnp.bfloat16, jnp.int32
    shape = jax.ShapeDtypeStruct
    vmem = pl.BlockSpec(memory_space=pltpu.VMEM)
    smem = pl.BlockSpec(memory_space=pltpu.SMEM)
    hbm = pl.BlockSpec(memory_space=pl.ANY)
    dma = pltpu.SemaphoreType.DMA
    with jax.named_scope("exchange_and_sweeps"):
        rx, ids, a_rows, b_rows, source_dual, target_dual = pl.pallas_call(
            functools.partial(exchange_kernel, n, blocks, half, scale),
            out_shape=(
                shape((reps, n, BLOCK, dim), bf16),
                shape((reps, n, BLOCK), i32),
                shape((reps, n, BLOCK), f32),
                shape((blocks, BLOCK), f32),
                shape((blocks, BLOCK), f32),
                shape((blocks, BLOCK), f32),
            ),
            in_specs=[smem, smem, hbm, hbm],
            out_specs=(hbm, vmem, vmem, vmem, vmem, vmem),
            scratch_shapes=[
                pltpu.VMEM((blocks, BLOCK, dim), bf16),
                pltpu.VMEM((blocks, BLOCK, dim), bf16),
                pltpu.VMEM((n, BLOCK, dim), bf16),
                pltpu.VMEM((n, BLOCK, dim), bf16),
                pltpu.VMEM((n, BLOCK, BLOCK), f32),
                pltpu.VMEM((n, BLOCK, BLOCK), f32),
                pltpu.VMEM((blocks, BLOCK, BLOCK), f32),
                pltpu.VMEM((n, 1, BLOCK), i32),
                pltpu.VMEM((n, 1, BLOCK), i32),
                pltpu.VMEM((reps, n, BLOCK), i32),
                pltpu.SMEM((n, 1, BLOCK), i32),
                pltpu.VMEM((n, BLOCK), i32),
                pltpu.VMEM((reps, n, BLOCK), i32),
                pltpu.VMEM((ITERS, n, 2, BLOCK), f32),
                pltpu.VMEM((ITERS, reps, n, 2, BLOCK), f32),
                pltpu.VMEM((reps, n, BLOCK), f32),
                pltpu.VMEM((reps, n, BLOCK), f32),
                pltpu.VMEM((blocks, BLOCK), f32),
                pltpu.VMEM((ITERS, n, 1, BLOCK), f32),
                pltpu.VMEM((ITERS, n, 1, BLOCK), f32),
                pltpu.VMEM((n, BLOCK), f32),
                pltpu.VMEM((reps, n, BLOCK), f32),
                pltpu.VMEM((reps, half, BLOCK), f32),
                pltpu.VMEM((-(-half // 8) * 8, BLOCK), f32),
                pltpu.VMEM((blocks, BLOCK), f32),
                pltpu.VMEM((blocks, BLOCK), f32),
                dma((3,)),
                dma((n,)), dma((n,)), dma((n,)), dma((n,)), dma((n,)), dma((n,)), dma((n,)),
                dma((ITERS, reps, n)), dma((ITERS, reps, n)), dma((ITERS, n)), dma((ITERS, n)),
                dma((4,)), dma((4,)),
            ],
            compiler_params=pltpu.CompilerParams(
                collective_id=0, has_side_effects=True, vmem_limit_bytes=VMEM_BYTES
            ),
            name="exchange_and_sweeps",
        )(picked, wanted, src, tgt)
    pairs = reps * n
    with jax.named_scope("gradient"):
        grad = pl.pallas_call(
            functools.partial(gradient_kernel, pairs, blocks, scale),
            out_shape=shape((blocks, BLOCK, dim), f32),
            in_specs=[smem, hbm, vmem, vmem, vmem],
            out_specs=hbm,
            scratch_shapes=[
                pltpu.VMEM((pairs, BLOCK, dim), bf16),
                pltpu.VMEM((blocks, BLOCK, dim), f32),
                pltpu.VMEM((blocks, BLOCK, BLOCK), f32),
                pltpu.VMEM((blocks, BLOCK, BLOCK), f32),
                dma((pairs // 4,)),
                dma((blocks,)),
            ],
            compiler_params=pltpu.CompilerParams(vmem_limit_bytes=VMEM_BYTES),
            name="gradient",
        )(
            ids.reshape(pairs, BLOCK),
            rx.reshape(pairs, BLOCK, dim),
            a_rows.reshape(pairs, BLOCK),
            b_rows,
            tgt,
        )
    return source_dual.reshape(-1), target_dual.reshape(-1), grad.reshape(rows, dim)


def solution(mesh):
    return jax.shard_map(
        on_device,
        mesh=mesh,
        in_specs=(
            P("pts", None),
            P("pts", None),
            P(("pts", "rep")),
            P(("pts", "rep")),
            P(("pts", "rep")),
        ),
        out_specs=(P("pts"), P("pts"), P("pts", None)),
        check_vma=False,
    )
```

```python
import functools

import jax
import jax.numpy as jnp
from jax import lax
from jax.experimental import pallas as pl
from jax.experimental.pallas import tpu as pltpu
from jax.sharding import PartitionSpec as P

BLOCK = 128
ITERS = 3
EPSILON = 0.05
NEG_BIG = -1e30
MESH = pl.DeviceIdType.MESH
VMEM_BYTES = 56 * 1024 * 1024


def loop(lower, upper, body):
    def step(i, carry):
        body(i)
        return carry

    lax.fori_loop(lower, upper, step, 0)


def grouped(total, size, body):
    def step(i):
        for k in range(size):
            body(i * size + k)

    loop(0, total // size, step)


def flipped(me, d, n):
    if n & (n - 1):
        return lax.rem(me + d, n)
    out, bit = 0, 1
    while bit < n:
        out = out + bit * (((me // bit) + (d // bit)) % 2)
        bit *= 2
    return out


def as_column(row):
    return jnp.transpose(jnp.broadcast_to(row, (BLOCK, BLOCK)))


def columns_of(rows):
    turned = jnp.transpose(rows)
    return [jnp.broadcast_to(turned[:, k:k + 1], (BLOCK, BLOCK)) for k in range(rows.shape[0])]


def square_row(block):
    values = block.astype(jnp.float32)
    column = jnp.sum(values * values, axis=1, keepdims=True)
    return jnp.transpose(jnp.broadcast_to(column, (BLOCK, BLOCK)))[0:1, :]


def logsum(terms):
    top = jnp.max(terms, axis=0, keepdims=True)
    return top + jnp.log(jnp.sum(jnp.exp(terms - top), axis=0, keepdims=True))


def combine(values, keys, key):
    return logsum(jnp.where(keys == key, values, NEG_BIG))


def in_turn(t, n):
    return jnp.where(t % 2 == 0, n // 2 + t // 2, lax.rem((t + 1) // 2, n // 2))


def exchange_kernel(
    n, blocks, half, scale,
    pair_source, pair_target, pair_count, src_hbm, tgt_hbm,
    rx_out, ids_out, a_out, b_out, source_out, target_out,
    src, tgt, out_x, rx, score, score_t, b_col, want_rows, ids_in, ids_all, ids_smem, id_keys,
    source_pick, wanted, source_keys, stats_out, stats_in, stat_rows, rep_out, rep_in, a_src, a_send, a_in, a_rows, a_all, b_all,
    b_pad, x_sq, y_sq,
    load_sem, x_send, x_recv, id_send, id_recv, fwd_send, fwd_recv, keep_sem,
    stat_send, stat_recv, a_ssem, a_rsem, rep_send, rep_recv, tail_send, tail_recv,
):
    me = lax.axis_index("pts")
    side = lax.axis_index("rep")
    other = 1 - side
    first = side * half

    load_src = pltpu.make_async_copy(src_hbm, src, load_sem.at[0])
    load_tgt = pltpu.make_async_copy(tgt_hbm, tgt, load_sem.at[1])
    load_src.start()
    load_tgt.start()

    barrier = pltpu.get_barrier_semaphore()

    def greet(d):
        pl.semaphore_signal(
            barrier, inc=1, device_id=(lax.rem(me + d, n), side), device_id_type=MESH
        )

    loop(1, n, greet)
    pl.semaphore_signal(barrier, inc=1, device_id=(me, other), device_id_type=MESH)

    slots = pair_source.shape[0]
    count = pair_count[0]

    def list_row(p):
        def look(k, found):
            offset = pair_target[k] - p * blocks
            mine = (k < count) & (offset >= 0) & (offset < blocks)
            local_source = pair_source[k] - me * blocks
            return jnp.where(mine, local_source, found[0]), jnp.where(mine, offset, found[1])

        found = (jnp.int32(-1), jnp.int32(-1))
        if slots <= 16:
            for k in range(slots):
                found = look(k, found)
        else:
            found = lax.fori_loop(0, slots, look, found)
        source_pick[p], wanted[p] = found
        want_rows[p] = jnp.full((1, BLOCK), found[1], jnp.int32)
        source_keys[pl.ds(p, 1), :] = jnp.full((1, BLOCK), found[0], jnp.int32)

    loop(0, n, list_row)
    pl.semaphore_wait(barrier, n)

    def to_peer(src_ref, dst_ref, send_sem, recv_sem, peer):
        return pltpu.make_async_remote_copy(
            src_ref=src_ref, dst_ref=dst_ref, send_sem=send_sem, recv_sem=recv_sem,
            device_id=(peer, side), device_id_type=MESH,
        )

    def to_twin(src_ref, dst_ref, send_sem, recv_sem):
        return pltpu.make_async_remote_copy(
            src_ref=src_ref, dst_ref=dst_ref, send_sem=send_sem, recv_sem=recv_sem,
            device_id=(me, other), device_id_type=MESH,
        )

    def id_copy(peer, slot):
        return to_peer(want_rows.at[peer], ids_in.at[slot], id_send.at[peer], id_recv.at[slot], peer)

    def x_copy(peer, slot):
        return to_peer(out_x.at[peer], rx.at[slot], x_send.at[peer], x_recv.at[slot], peer)

    def stat_copy(it, peer, slot):
        return to_peer(
            stats_out.at[it, peer], stats_in.at[it, slot],
            stat_send.at[it, peer], stat_recv.at[it, slot], peer,
        )

    def swap(it):
        return to_twin(rep_out.at[it], rep_in.at[it], rep_send.at[it], rep_recv.at[it])

    def a_copy(it, peer, slot):
        return to_peer(
            a_send.at[it, peer], a_in.at[it, slot], a_ssem.at[it, peer], a_rsem.at[it, slot], peer
        )

    def keep_copy(slot):
        return pltpu.make_async_copy(rx.at[slot], rx_out.at[side, slot], keep_sem.at[slot])

    def forward_copy(slot, which):
        return to_twin(
            rx.at[slot], rx_out.at[which, slot], fwd_send.at[slot], fwd_recv.at[slot]
        )

    def tail_copy(k, ref, which):
        return to_twin(ref.at[which], ref.at[which], tail_send.at[k], tail_recv.at[k])

    loop(1, n, lambda d: id_copy(lax.rem(me + d, n), me).start())
    load_src.wait()

    def send_block(d):
        peer = flipped(me, d, n)
        out_x[peer] = src[jnp.maximum(source_pick[peer], 0)]
        x_copy(peer, me).start()

    loop(0, n - 1, lambda t: send_block(in_turn(t, n)))
    rx[me] = src[jnp.maximum(source_pick[me], 0)]
    ids_in[me] = want_rows[me]
    load_tgt.wait()
    b_pad[...] = jnp.zeros(b_pad.shape, jnp.float32)

    def source_squares(b):
        x_sq[pl.ds(b, 1), :] = scale * square_row(src[b])

    def target_squares(b):
        row = scale * square_row(tgt[b])
        y_sq[pl.ds(b, 1), :] = row
        b_col[b] = as_column(-row)

    loop(0, blocks, source_squares)
    loop(0, blocks, target_squares)

    def take_id(d):
        peer = lax.rem(me + d, n)
        id_copy(peer, peer).wait_recv()

    loop(1, n, take_id)
    ids_move = pltpu.make_async_copy(ids_in, ids_smem, load_sem.at[2])
    ids_move.start()

    def id_row(q):
        row = ids_in[q]
        id_keys[pl.ds(q, 1), :] = row
        ids_all[side, pl.ds(q, 1), :] = row

    loop(0, n, id_row)
    tail_copy(0, ids_all, side).start()
    ids_move.wait()

    def local_id(q):
        return jnp.maximum(ids_smem[q, 0, 0], 0)

    def arrivals(group):
        offsets = [in_turn(group * 4 + k, n) for k in range(4)]
        peers = [flipped(me, d, n) for d in offsets]
        for d, peer in zip(offsets, peers):
            @pl.when(d > 0)
            def _():
                x_copy(peer, peer).wait_recv()

        for peer in peers:
            pick = local_id(peer)
            grid = lax.dot_general(
                rx[peer], tgt[pick], (((1,), (1,)), ((), ())), preferred_element_type=jnp.float32
            ) * (2.0 * scale)
            grid_t = jnp.transpose(grid)
            score[peer] = grid
            score_t[peer] = grid_t
            stats_out[0, peer] = logsum(b_col[pick] + grid_t)
        for d, peer in zip(offsets, peers):
            @pl.when(d > 0)
            def _():
                stat_copy(0, peer, me).start()

        for peer in peers:
            keep_copy(peer).start()
            forward_copy(peer, side).start()

    loop(0, n // 4, arrivals)

    for it in range(ITERS):
        def take_stats(d):
            peer = lax.rem(me + d, n)
            stat_copy(it, peer, peer).wait_recv()

        loop(1, n, take_stats)
        stats_in[it, me] = stats_out[it, me]

        def stat_row(p):
            stat_rows[pl.ds(p, 1), :] = stats_in[it, p]

        grouped(n, 8, stat_row)
        values, keys = stat_rows[...], source_keys[...]
        for b in range(blocks):
            rep_out[it, b:b + 1, :] = combine(values, keys, b)
        swap(it).start()
        swap(it).wait_recv()
        top = jnp.maximum(rep_out[it], rep_in[it])
        total = jnp.exp(rep_out[it] - top) + jnp.exp(rep_in[it] - top)
        a_src[...] = -(top + jnp.log(total))

        def send_a(d):
            peer = lax.rem(me + d, n)
            a_send[it, peer] = a_src[pl.ds(jnp.maximum(source_pick[peer], 0), 1), :]
            a_copy(it, peer, me).start()

        loop(1, n, send_a)
        a_in[it, me] = a_src[pl.ds(jnp.maximum(source_pick[me], 0), 1), :]

        def take_a(d):
            peer = lax.rem(me + d, n)
            a_copy(it, peer, peer).wait_recv()

        loop(1, n, take_a)

        def a_row(q):
            a_rows[pl.ds(q, 1), :] = a_in[it, q]

        grouped(n, 8, a_row)
        if it + 1 == ITERS:
            a_all[side] = a_rows[...]
            tail_copy(1, a_all, side).start()

        def column_visits(chunk):
            base = chunk * 16
            for k, column in enumerate(columns_of(a_rows[pl.ds(pl.multiple_of(base, 16), 16), :])):
                stat_rows[pl.ds(base + k, 1), :] = logsum(column + score[base + k])

        loop(0, n // 16, column_visits)
        values, keys = stat_rows[...], id_keys[...]
        for b in range(half):
            b_pad[b:b + 1, :] = -combine(values, keys, b + first)
        if it + 1 == ITERS:
            b_all[side] = b_pad[0:half, :]
        else:
            for b, column in enumerate(columns_of(b_pad[...])[:half]):
                b_col[first + b] = column

            def next_rows(group):
                for k in range(4):
                    q = lax.rem(me + group * 4 + k, n)
                    stats_out[it + 1, q] = logsum(b_col[local_id(q)] + score_t[q])
                for k in range(4):
                    d = group * 4 + k

                    @pl.when(d > 0)
                    def _():
                        stat_copy(it + 1, lax.rem(me + d, n), me).start()

            loop(0, n // 4, next_rows)

    tail_copy(2, b_all, side).start()
    source_out[...] = EPSILON * (a_src[...] + x_sq[...])

    def finish_local(q):
        keep_copy(q).wait()
        forward_copy(q, other).wait_recv()
        forward_copy(q, side).wait_send()

    loop(0, n, finish_local)

    def finish_sends(d):
        peer = lax.rem(me + d, n)
        id_copy(peer, me).wait_send()
        x_copy(peer, me).wait_send()
        for it in range(ITERS):
            stat_copy(it, peer, me).wait_send()
            a_copy(it, peer, me).wait_send()

    loop(1, n, finish_sends)
    for it in range(ITERS):
        swap(it).wait_send()
    for k, ref in enumerate((ids_all, a_all, b_all)):
        tail_copy(k, ref, other).wait_recv()
        tail_copy(k, ref, side).wait_send()
    ids_out[...] = ids_all[...]
    a_out[...] = a_all[...]
    for part in range(2):
        b_out[part * half:(part + 1) * half, :] = b_all[part]
    target_out[...] = EPSILON * (b_out[...] + y_sq[...])


def gradient_kernel(
    pairs, blocks, scale, ids, rx_hbm, a_rows, b_rows, tgt, source_in, target_in,
    out, source_out, target_out, rx, grad, b_col, mass, sems, out_sems,
):
    groups = pairs // 4

    def fetch(group):
        part = pl.ds(group * 4, 4)
        return pltpu.make_async_copy(rx_hbm.at[part], rx.at[part], sems.at[group])

    def store(b):
        return pltpu.make_async_copy(grad.at[b], out.at[b], out_sems.at[b])

    loop(0, groups, lambda group: fetch(group).start())
    source_out[...] = source_in[...]
    target_out[...] = target_in[...]
    for b, column in enumerate(columns_of(b_rows[...])):
        b_col[b] = column

    def prepare(b):
        grad[b] = jnp.zeros(grad.shape[1:], jnp.float32)
        mass[b] = jnp.zeros((BLOCK, BLOCK), jnp.float32)

    grouped(blocks, 4, prepare)

    def visit(group):
        fetch(group).wait()
        results = []
        for k in range(4):
            q = group * 4 + k
            target = ids[q, 0]
            pick = jnp.maximum(target, 0)
            grid = lax.dot_general(
                tgt[pick], rx[q], (((1,), (1,)), ((), ())), preferred_element_type=jnp.float32
            ) * (2.0 * scale)
            plan = jnp.exp(b_col[pick] + (grid + a_rows[pl.ds(q, 1), :]))
            plan = jnp.where(target >= 0, plan, 0.0)
            part = jnp.dot(plan.astype(jnp.bfloat16), rx[q], preferred_element_type=jnp.float32)
            results.append((pick, plan, part))
        for pick, plan, part in results:
            grad[pick] += part
            mass[pick] += plan

    loop(0, groups, visit)

    def finish(group):
        for k in range(4):
            b = group * 4 + k
            column = jnp.sum(mass[b], axis=1, keepdims=True)
            grad[b] = tgt[b].astype(jnp.float32) * column - grad[b]
        for k in range(4):
            store(group * 4 + k).start()

    loop(0, blocks // 4, finish)
    loop(0, blocks, lambda b: store(b).wait())


def on_device(src_points, tgt_points, pair_source, pair_target, pair_count):
    n = lax.axis_size("pts")
    reps = lax.axis_size("rep")
    rows, dim = src_points.shape
    blocks = rows // BLOCK
    half = blocks // reps
    scale = 1.0 / EPSILON / dim
    src = src_points.reshape(blocks, BLOCK, dim)
    tgt = tgt_points.reshape(blocks, BLOCK, dim)

    f32, bf16, i32 = jnp.float32, jnp.bfloat16, jnp.int32
    shape = jax.ShapeDtypeStruct
    vmem = pl.BlockSpec(memory_space=pltpu.VMEM)
    smem = pl.BlockSpec(memory_space=pltpu.SMEM)
    hbm = pl.BlockSpec(memory_space=pl.ANY)
    dma = pltpu.SemaphoreType.DMA
    with jax.named_scope("exchange_and_sweeps"):
        rx, ids, a_rows, b_rows, source_dual, target_dual = pl.pallas_call(
            functools.partial(exchange_kernel, n, blocks, half, scale),
            out_shape=(
                shape((reps, n, BLOCK, dim), bf16),
                shape((reps, n, BLOCK), i32),
                shape((reps, n, BLOCK), f32),
                shape((blocks, BLOCK), f32),
                shape((blocks, BLOCK), f32),
                shape((blocks, BLOCK), f32),
            ),
            in_specs=[smem, smem, smem, hbm, hbm],
            out_specs=(hbm, vmem, vmem, vmem, vmem, vmem),
            scratch_shapes=[
                pltpu.VMEM((blocks, BLOCK, dim), bf16),
                pltpu.VMEM((blocks, BLOCK, dim), bf16),
                pltpu.VMEM((n, BLOCK, dim), bf16),
                pltpu.VMEM((n, BLOCK, dim), bf16),
                pltpu.VMEM((n, BLOCK, BLOCK), f32),
                pltpu.VMEM((n, BLOCK, BLOCK), f32),
                pltpu.VMEM((blocks, BLOCK, BLOCK), f32),
                pltpu.VMEM((n, 1, BLOCK), i32),
                pltpu.VMEM((n, 1, BLOCK), i32),
                pltpu.VMEM((reps, n, BLOCK), i32),
                pltpu.SMEM((n, 1, BLOCK), i32),
                pltpu.VMEM((n, BLOCK), i32),
                pltpu.SMEM((n,), i32),
                pltpu.SMEM((n,), i32),
                pltpu.VMEM((n, BLOCK), i32),
                pltpu.VMEM((ITERS, n, 1, BLOCK), f32),
                pltpu.VMEM((ITERS, n, 1, BLOCK), f32),
                pltpu.VMEM((n, BLOCK), f32),
                pltpu.VMEM((ITERS, blocks, BLOCK), f32),
                pltpu.VMEM((ITERS, blocks, BLOCK), f32),
                pltpu.VMEM((blocks, BLOCK), f32),
                pltpu.VMEM((ITERS, n, 1, BLOCK), f32),
                pltpu.VMEM((ITERS, n, 1, BLOCK), f32),
                pltpu.VMEM((n, BLOCK), f32),
                pltpu.VMEM((reps, n, BLOCK), f32),
                pltpu.VMEM((reps, half, BLOCK), f32),
                pltpu.VMEM((-(-half // 8) * 8, BLOCK), f32),
                pltpu.VMEM((blocks, BLOCK), f32),
                pltpu.VMEM((blocks, BLOCK), f32),
                dma((3,)),
                dma((n,)), dma((n,)), dma((n,)), dma((n,)), dma((n,)), dma((n,)), dma((n,)),
                dma((ITERS, n)), dma((ITERS, n)), dma((ITERS, n)), dma((ITERS, n)),
                dma((ITERS,)), dma((ITERS,)), dma((3,)), dma((3,)),
            ],
            compiler_params=pltpu.CompilerParams(
                collective_id=0, has_side_effects=True, vmem_limit_bytes=VMEM_BYTES
            ),
            name="exchange_and_sweeps",
        )(pair_source, pair_target, pair_count, src, tgt)
    pairs = reps * n
    with jax.named_scope("gradient"):
        grad, source_dual, target_dual = pl.pallas_call(
            functools.partial(gradient_kernel, pairs, blocks, scale),
            out_shape=(
                shape((blocks, BLOCK, dim), f32),
                shape((blocks, BLOCK), f32),
                shape((blocks, BLOCK), f32),
            ),
            in_specs=[smem, hbm, vmem, vmem, vmem, vmem, vmem],
            out_specs=(hbm, vmem, vmem),
            scratch_shapes=[
                pltpu.VMEM((pairs, BLOCK, dim), bf16),
                pltpu.VMEM((blocks, BLOCK, dim), f32),
                pltpu.VMEM((blocks, BLOCK, BLOCK), f32),
                pltpu.VMEM((blocks, BLOCK, BLOCK), f32),
                dma((pairs // 4,)),
                dma((blocks,)),
            ],
            compiler_params=pltpu.CompilerParams(vmem_limit_bytes=VMEM_BYTES),
            name="gradient",
        )(
            ids.reshape(pairs, BLOCK),
            rx.reshape(pairs, BLOCK, dim),
            a_rows.reshape(pairs, BLOCK),
            b_rows,
            tgt,
            source_dual,
            target_dual,
        )
    return source_dual.reshape(-1), target_dual.reshape(-1), grad.reshape(rows, dim)


def solution(mesh):
    return jax.shard_map(
        on_device,
        mesh=mesh,
        in_specs=(
            P("pts", None),
            P("pts", None),
            P(("pts", "rep")),
            P(("pts", "rep")),
            P(("pts", "rep")),
        ),
        out_specs=(P("pts"), P("pts"), P("pts", None)),
        check_vma=False,
    )
```

```python
import functools

import jax
import jax.numpy as jnp
from jax import lax
from jax.experimental import pallas as pl
from jax.experimental.pallas import tpu as pltpu
from jax.sharding import PartitionSpec as P

BLOCK = 128
ITERS = 3
EPSILON = 0.05
NEG_BIG = -1e30
MESH = pl.DeviceIdType.MESH
VMEM_BYTES = 56 * 1024 * 1024


def loop(lower, upper, body):
    def step(i, carry):
        body(i)
        return carry

    lax.fori_loop(lower, upper, step, 0)


def grouped(total, size, body):
    def step(i):
        for k in range(size):
            body(i * size + k)

    loop(0, total // size, step)


def flipped(me, d, n):
    if n & (n - 1):
        return lax.rem(me + d, n)
    out, bit = 0, 1
    while bit < n:
        out = out + bit * (((me // bit) + (d // bit)) % 2)
        bit *= 2
    return out


def as_column(row):
    return jnp.transpose(jnp.broadcast_to(row, (BLOCK, BLOCK)))


def columns_of(rows):
    turned = jnp.transpose(rows)
    return [jnp.broadcast_to(turned[:, k:k + 1], (BLOCK, BLOCK)) for k in range(rows.shape[0])]


def square_row(block):
    values = block.astype(jnp.float32)
    column = jnp.sum(values * values, axis=1, keepdims=True)
    return jnp.transpose(jnp.broadcast_to(column, (BLOCK, BLOCK)))[0:1, :]


def logsum(terms):
    top = jnp.max(terms, axis=0, keepdims=True)
    return top + jnp.log(jnp.sum(jnp.exp(terms - top), axis=0, keepdims=True))


def combine(values, keys, key):
    return logsum(jnp.where(keys == key, values, NEG_BIG))


def in_turn(t, n):
    return jnp.where(t % 2 == 0, n // 2 + t // 2, lax.rem((t + 1) // 2, n // 2))


def exchange_kernel(
    n, blocks, half, scale,
    pair_source, pair_target, pair_count, src_hbm, tgt_hbm,
    rx_out, ids_out, a_out, b_out, source_out, target_out,
    src, tgt, out_x, rx, score, score_t, b_col, want_rows, ids_in, ids_all, ids_smem, id_keys,
    source_pick, wanted, source_keys, stats_out, stats_in, stat_rows, rep_out, rep_in, a_src, a_send, a_in, a_rows, a_all, b_all,
    b_pad, x_sq, y_sq,
    load_sem, x_send, x_recv, id_send, id_recv, fwd_send, fwd_recv, keep_sem,
    stat_send, stat_recv, a_ssem, a_rsem, rep_send, rep_recv, tail_send, tail_recv,
):
    me = lax.axis_index("pts")
    side = lax.axis_index("rep")
    other = 1 - side
    first = side * half

    load_src = pltpu.make_async_copy(src_hbm, src, load_sem.at[0])
    load_tgt = pltpu.make_async_copy(tgt_hbm, tgt, load_sem.at[1])
    load_src.start()
    load_tgt.start()

    barrier = pltpu.get_barrier_semaphore()

    def greet(d):
        pl.semaphore_signal(
            barrier, inc=1, device_id=(lax.rem(me + d, n), side), device_id_type=MESH
        )

    loop(1, n, greet)
    pl.semaphore_signal(barrier, inc=1, device_id=(me, other), device_id_type=MESH)

    slots = pair_source.shape[0]
    count = pair_count[0]

    def list_row(p):
        def look(k, found):
            offset = pair_target[k] - p * blocks
            mine = (k < count) & (offset >= 0) & (offset < blocks)
            local_source = pair_source[k] - me * blocks
            return jnp.where(mine, local_source, found[0]), jnp.where(mine, offset, found[1])

        found = (jnp.int32(-1), jnp.int32(-1))
        if slots <= 16:
            for k in range(slots):
                found = look(k, found)
        else:
            found = lax.fori_loop(0, slots, look, found)
        source_pick[p], wanted[p] = found
        want_rows[p] = jnp.full((1, BLOCK), found[1], jnp.int32)
        source_keys[pl.ds(p, 1), :] = jnp.full((1, BLOCK), found[0], jnp.int32)

    loop(0, n, list_row)
    pl.semaphore_wait(barrier, n)

    def to_peer(src_ref, dst_ref, send_sem, recv_sem, peer):
        return pltpu.make_async_remote_copy(
            src_ref=src_ref, dst_ref=dst_ref, send_sem=send_sem, recv_sem=recv_sem,
            device_id=(peer, side), device_id_type=MESH,
        )

    def to_twin(src_ref, dst_ref, send_sem, recv_sem):
        return pltpu.make_async_remote_copy(
            src_ref=src_ref, dst_ref=dst_ref, send_sem=send_sem, recv_sem=recv_sem,
            device_id=(me, other), device_id_type=MESH,
        )

    def id_copy(peer, slot):
        return to_peer(want_rows.at[peer], ids_in.at[slot], id_send.at[peer], id_recv.at[slot], peer)

    def x_copy(peer, slot):
        return to_peer(out_x.at[peer], rx.at[slot], x_send.at[peer], x_recv.at[slot], peer)

    def stat_copy(it, peer, slot):
        return to_peer(
            stats_out.at[it, peer], stats_in.at[it, slot],
            stat_send.at[it, peer], stat_recv.at[it, slot], peer,
        )

    def swap(it):
        return to_twin(rep_out.at[it], rep_in.at[it], rep_send.at[it], rep_recv.at[it])

    def a_copy(it, peer, slot):
        return to_peer(
            a_send.at[it, peer], a_in.at[it, slot], a_ssem.at[it, peer], a_rsem.at[it, slot], peer
        )

    def keep_copy(slot):
        return pltpu.make_async_copy(rx.at[slot], rx_out.at[side, slot], keep_sem.at[slot])

    def forward_copy(slot, which):
        return to_twin(
            rx.at[slot], rx_out.at[which, slot], fwd_send.at[slot], fwd_recv.at[slot]
        )

    def tail_copy(k, ref, which):
        return to_twin(ref.at[which], ref.at[which], tail_send.at[k], tail_recv.at[k])

    loop(1, n, lambda d: id_copy(lax.rem(me + d, n), me).start())
    load_src.wait()

    def send_block(d):
        peer = flipped(me, d, n)
        out_x[peer] = src[jnp.maximum(source_pick[peer], 0)]
        x_copy(peer, me).start()

    loop(0, n - 1, lambda t: send_block(in_turn(t, n)))
    rx[me] = src[jnp.maximum(source_pick[me], 0)]
    ids_in[me] = want_rows[me]
    load_tgt.wait()
    b_pad[...] = jnp.zeros(b_pad.shape, jnp.float32)

    def source_squares(b):
        x_sq[pl.ds(b, 1), :] = scale * square_row(src[b])

    def target_squares(b):
        row = scale * square_row(tgt[b])
        y_sq[pl.ds(b, 1), :] = row
        b_col[b] = as_column(-row)

    loop(0, blocks, source_squares)
    loop(0, blocks, target_squares)

    def take_id(d):
        peer = lax.rem(me + d, n)
        id_copy(peer, peer).wait_recv()

    loop(1, n, take_id)
    ids_move = pltpu.make_async_copy(ids_in, ids_smem, load_sem.at[2])
    ids_move.start()

    def id_row(q):
        row = ids_in[q]
        id_keys[pl.ds(q, 1), :] = row
        ids_all[side, pl.ds(q, 1), :] = row

    loop(0, n, id_row)
    tail_copy(0, ids_all, side).start()
    ids_move.wait()

    def local_id(q):
        return jnp.maximum(ids_smem[q, 0, 0], 0)

    def arrivals(group):
        offsets = [in_turn(group * 4 + k, n) for k in range(4)]
        peers = [flipped(me, d, n) for d in offsets]
        for d, peer in zip(offsets, peers):
            @pl.when(d > 0)
            def _():
                x_copy(peer, peer).wait_recv()

        picks = [local_id(peer) for peer in peers]
        grids = [
            lax.dot_general(
                rx[peer], tgt[pick], (((1,), (1,)), ((), ())), preferred_element_type=jnp.float32
            ) * (2.0 * scale)
            for peer, pick in zip(peers, picks)
        ]
        turned = [jnp.transpose(grid) for grid in grids]
        rows = [logsum(b_col[pick] + grid_t) for pick, grid_t in zip(picks, turned)]
        for peer, row in zip(peers, rows):
            stats_out[0, peer] = row
        for d, peer in zip(offsets, peers):
            @pl.when(d > 0)
            def _():
                stat_copy(0, peer, me).start()

        for peer, grid, grid_t in zip(peers, grids, turned):
            score[peer] = grid
            score_t[peer] = grid_t
        for peer in peers:
            keep_copy(peer).start()
            forward_copy(peer, side).start()

    loop(0, n // 4, arrivals)

    for it in range(ITERS):
        def take_stats(d):
            peer = lax.rem(me + d, n)
            stat_copy(it, peer, peer).wait_recv()

        loop(1, n, take_stats)
        stats_in[it, me] = stats_out[it, me]

        def stat_row(p):
            stat_rows[pl.ds(p, 1), :] = stats_in[it, p]

        grouped(n, 8, stat_row)
        values, keys = stat_rows[...], source_keys[...]
        rows = [combine(values, keys, b) for b in range(blocks)]
        for b, row in enumerate(rows):
            rep_out[it, b:b + 1, :] = row
        swap(it).start()
        swap(it).wait_recv()
        top = jnp.maximum(rep_out[it], rep_in[it])
        total = jnp.exp(rep_out[it] - top) + jnp.exp(rep_in[it] - top)
        a_src[...] = -(top + jnp.log(total))

        def send_a(d):
            peer = lax.rem(me + n // 2 + d, n)
            a_send[it, peer] = a_src[pl.ds(jnp.maximum(source_pick[peer], 0), 1), :]
            a_copy(it, peer, me).start()

        loop(0, n // 2, send_a)
        loop(n // 2 + 1, n, send_a)
        a_in[it, me] = a_src[pl.ds(jnp.maximum(source_pick[me], 0), 1), :]

        def take_a(d):
            peer = lax.rem(me + d, n)
            a_copy(it, peer, peer).wait_recv()

        loop(1, n, take_a)

        def a_row(q):
            a_rows[pl.ds(q, 1), :] = a_in[it, q]

        grouped(n, 8, a_row)
        if it + 1 == ITERS:
            a_all[side] = a_rows[...]
            tail_copy(1, a_all, side).start()

        def column_visits(chunk):
            base = chunk * 16
            columns = columns_of(a_rows[pl.ds(pl.multiple_of(base, 16), 16), :])
            rows = [logsum(column + score[base + k]) for k, column in enumerate(columns)]
            for k, row in enumerate(rows):
                stat_rows[pl.ds(base + k, 1), :] = row

        loop(0, n // 16, column_visits)
        values, keys = stat_rows[...], id_keys[...]
        rows = [-combine(values, keys, b + first) for b in range(half)]
        for b, row in enumerate(rows):
            b_pad[b:b + 1, :] = row
        if it + 1 == ITERS:
            b_all[side] = b_pad[0:half, :]
        else:
            for b, column in enumerate(columns_of(b_pad[...])[:half]):
                b_col[first + b] = column

            def next_rows(group):
                peers = [lax.rem(me + n // 2 + group * 8 + k, n) for k in range(8)]
                rows = [logsum(b_col[local_id(q)] + score_t[q]) for q in peers]
                for q, row in zip(peers, rows):
                    stats_out[it + 1, q] = row
                for q in peers:
                    @pl.when(q != me)
                    def _():
                        stat_copy(it + 1, q, me).start()

            loop(0, n // 8, next_rows)

    tail_copy(2, b_all, side).start()
    source_out[...] = EPSILON * (a_src[...] + x_sq[...])

    def finish_local(q):
        keep_copy(q).wait()
        forward_copy(q, other).wait_recv()
        forward_copy(q, side).wait_send()

    loop(0, n, finish_local)

    def finish_sends(d):
        peer = lax.rem(me + d, n)
        id_copy(peer, me).wait_send()
        x_copy(peer, me).wait_send()
        for it in range(ITERS):
            stat_copy(it, peer, me).wait_send()
            a_copy(it, peer, me).wait_send()

    loop(1, n, finish_sends)
    for it in range(ITERS):
        swap(it).wait_send()
    for k, ref in enumerate((ids_all, a_all, b_all)):
        tail_copy(k, ref, other).wait_recv()
        tail_copy(k, ref, side).wait_send()
    ids_out[...] = ids_all[...]
    a_out[...] = a_all[...]
    for part in range(2):
        b_out[part * half:(part + 1) * half, :] = b_all[part]
    target_out[...] = EPSILON * (b_out[...] + y_sq[...])


def gradient_kernel(
    pairs, blocks, scale, ids, rx_hbm, a_rows, b_rows, tgt_hbm, source_in, target_in,
    out, source_out, target_out, rx, tgt, grad, b_col, mass, sems, out_sems,
):
    groups = pairs // 4

    def fetch(group):
        part = pl.ds(group * 4, 4)
        return pltpu.make_async_copy(rx_hbm.at[part], rx.at[part], sems.at[group])

    def store(b):
        return pltpu.make_async_copy(grad.at[b], out.at[b], out_sems.at[b])

    load_tgt = pltpu.make_async_copy(tgt_hbm, tgt, out_sems.at[blocks])
    load_tgt.start()
    loop(0, groups, lambda group: fetch(group).start())
    source_out[...] = source_in[...]
    target_out[...] = target_in[...]
    for b, column in enumerate(columns_of(b_rows[...])):
        b_col[b] = column

    def prepare(b):
        grad[b] = jnp.zeros(grad.shape[1:], jnp.float32)
        mass[b] = jnp.zeros((BLOCK, BLOCK), jnp.float32)

    grouped(blocks, 4, prepare)
    load_tgt.wait()

    def visit(group):
        fetch(group).wait()
        results = []
        for k in range(4):
            q = group * 4 + k
            target = ids[q, 0]
            pick = jnp.maximum(target, 0)
            grid = lax.dot_general(
                tgt[pick], rx[q], (((1,), (1,)), ((), ())), preferred_element_type=jnp.float32
            ) * (2.0 * scale)
            plan = jnp.exp(b_col[pick] + (grid + a_rows[pl.ds(q, 1), :]))
            plan = jnp.where(target >= 0, plan, 0.0)
            part = jnp.dot(plan.astype(jnp.bfloat16), rx[q], preferred_element_type=jnp.float32)
            results.append((pick, plan, part))
        for pick, plan, part in results:
            grad[pick] += part
            mass[pick] += plan

    loop(0, groups, visit)

    def finish(group):
        for k in range(4):
            b = group * 4 + k
            column = jnp.sum(mass[b], axis=1, keepdims=True)
            grad[b] = tgt[b].astype(jnp.float32) * column - grad[b]
        for k in range(4):
            store(group * 4 + k).start()

    loop(0, blocks // 4, finish)
    loop(0, blocks, lambda b: store(b).wait())


def on_device(src_points, tgt_points, pair_source, pair_target, pair_count):
    n = lax.axis_size("pts")
    reps = lax.axis_size("rep")
    rows, dim = src_points.shape
    blocks = rows // BLOCK
    half = blocks // reps
    scale = 1.0 / EPSILON / dim
    src = src_points.reshape(blocks, BLOCK, dim)
    tgt = tgt_points.reshape(blocks, BLOCK, dim)

    f32, bf16, i32 = jnp.float32, jnp.bfloat16, jnp.int32
    shape = jax.ShapeDtypeStruct
    vmem = pl.BlockSpec(memory_space=pltpu.VMEM)
    smem = pl.BlockSpec(memory_space=pltpu.SMEM)
    hbm = pl.BlockSpec(memory_space=pl.ANY)
    dma = pltpu.SemaphoreType.DMA
    with jax.named_scope("exchange_and_sweeps"):
        rx, ids, a_rows, b_rows, source_dual, target_dual = pl.pallas_call(
            functools.partial(exchange_kernel, n, blocks, half, scale),
            out_shape=(
                shape((reps, n, BLOCK, dim), bf16),
                shape((reps, n, BLOCK), i32),
                shape((reps, n, BLOCK), f32),
                shape((blocks, BLOCK), f32),
                shape((blocks, BLOCK), f32),
                shape((blocks, BLOCK), f32),
            ),
            in_specs=[smem, smem, smem, hbm, hbm],
            out_specs=(hbm, vmem, vmem, vmem, vmem, vmem),
            scratch_shapes=[
                pltpu.VMEM((blocks, BLOCK, dim), bf16),
                pltpu.VMEM((blocks, BLOCK, dim), bf16),
                pltpu.VMEM((n, BLOCK, dim), bf16),
                pltpu.VMEM((n, BLOCK, dim), bf16),
                pltpu.VMEM((n, BLOCK, BLOCK), f32),
                pltpu.VMEM((n, BLOCK, BLOCK), f32),
                pltpu.VMEM((blocks, BLOCK, BLOCK), f32),
                pltpu.VMEM((n, 1, BLOCK), i32),
                pltpu.VMEM((n, 1, BLOCK), i32),
                pltpu.VMEM((reps, n, BLOCK), i32),
                pltpu.SMEM((n, 1, BLOCK), i32),
                pltpu.VMEM((n, BLOCK), i32),
                pltpu.SMEM((n,), i32),
                pltpu.SMEM((n,), i32),
                pltpu.VMEM((n, BLOCK), i32),
                pltpu.VMEM((ITERS, n, 1, BLOCK), f32),
                pltpu.VMEM((ITERS, n, 1, BLOCK), f32),
                pltpu.VMEM((n, BLOCK), f32),
                pltpu.VMEM((ITERS, blocks, BLOCK), f32),
                pltpu.VMEM((ITERS, blocks, BLOCK), f32),
                pltpu.VMEM((blocks, BLOCK), f32),
                pltpu.VMEM((ITERS, n, 1, BLOCK), f32),
                pltpu.VMEM((ITERS, n, 1, BLOCK), f32),
                pltpu.VMEM((n, BLOCK), f32),
                pltpu.VMEM((reps, n, BLOCK), f32),
                pltpu.VMEM((reps, half, BLOCK), f32),
                pltpu.VMEM((-(-half // 8) * 8, BLOCK), f32),
                pltpu.VMEM((blocks, BLOCK), f32),
                pltpu.VMEM((blocks, BLOCK), f32),
                dma((3,)),
                dma((n,)), dma((n,)), dma((n,)), dma((n,)), dma((n,)), dma((n,)), dma((n,)),
                dma((ITERS, n)), dma((ITERS, n)), dma((ITERS, n)), dma((ITERS, n)),
                dma((ITERS,)), dma((ITERS,)), dma((3,)), dma((3,)),
            ],
            compiler_params=pltpu.CompilerParams(
                collective_id=0, has_side_effects=True, vmem_limit_bytes=VMEM_BYTES
            ),
            name="exchange_and_sweeps",
        )(pair_source, pair_target, pair_count, src, tgt)
    pairs = reps * n
    with jax.named_scope("gradient"):
        grad, source_dual, target_dual = pl.pallas_call(
            functools.partial(gradient_kernel, pairs, blocks, scale),
            out_shape=(
                shape((blocks, BLOCK, dim), f32),
                shape((blocks, BLOCK), f32),
                shape((blocks, BLOCK), f32),
            ),
            in_specs=[smem, hbm, vmem, vmem, hbm, vmem, vmem],
            out_specs=(hbm, vmem, vmem),
            scratch_shapes=[
                pltpu.VMEM((pairs, BLOCK, dim), bf16),
                pltpu.VMEM((blocks, BLOCK, dim), bf16),
                pltpu.VMEM((blocks, BLOCK, dim), f32),
                pltpu.VMEM((blocks, BLOCK, BLOCK), f32),
                pltpu.VMEM((blocks, BLOCK, BLOCK), f32),
                dma((pairs // 4,)),
                dma((blocks + 1,)),
            ],
            compiler_params=pltpu.CompilerParams(vmem_limit_bytes=VMEM_BYTES),
            name="gradient",
        )(
            ids.reshape(pairs, BLOCK),
            rx.reshape(pairs, BLOCK, dim),
            a_rows.reshape(pairs, BLOCK),
            b_rows,
            tgt,
            source_dual,
            target_dual,
        )
    return source_dual.reshape(-1), target_dual.reshape(-1), grad.reshape(rows, dim)


def solution(mesh):
    return jax.shard_map(
        on_device,
        mesh=mesh,
        in_specs=(
            P("pts", None),
            P("pts", None),
            P(("pts", "rep")),
            P(("pts", "rep")),
            P(("pts", "rep")),
        ),
        out_specs=(P("pts"), P("pts"), P("pts", None)),
        check_vma=False,
    )
```

```python
import functools

import jax
import jax.numpy as jnp
from jax import lax
from jax.experimental import pallas as pl
from jax.experimental.pallas import tpu as pltpu
from jax.sharding import PartitionSpec as P

BLOCK = 128
ITERS = 3
EPSILON = 0.05
NEG_BIG = -1e30
MESH = pl.DeviceIdType.MESH
VMEM_BYTES = 56 * 1024 * 1024


def loop(lower, upper, body):
    def step(i, carry):
        body(i)
        return carry

    lax.fori_loop(lower, upper, step, 0)


def spread(lower, upper, body):
    if upper - lower <= 16:
        for i in range(lower, upper):
            body(i)
    else:
        loop(lower, upper, body)


def unless_zero(d, action):
    if not isinstance(d, int):
        pl.when(d > 0)(action)
    elif d:
        action()


def grouped(total, size, body):
    def step(i):
        for k in range(size):
            body(i * size + k)

    loop(0, total // size, step)


def flipped(me, d, n):
    if n & (n - 1):
        return lax.rem(me + d, n)
    out, bit = 0, 1
    while bit < n:
        out = out + bit * (((me // bit) + (d // bit)) % 2)
        bit *= 2
    return out


def as_column(row):
    return jnp.transpose(jnp.broadcast_to(row, (BLOCK, BLOCK)))


def columns_of(rows):
    turned = jnp.transpose(rows)
    return [jnp.broadcast_to(turned[:, k:k + 1], (BLOCK, BLOCK)) for k in range(rows.shape[0])]


def square_row(block):
    values = block.astype(jnp.float32)
    column = jnp.sum(values * values, axis=1, keepdims=True)
    return jnp.transpose(jnp.broadcast_to(column, (BLOCK, BLOCK)))[0:1, :]


def logsum(terms):
    top = jnp.max(terms, axis=0, keepdims=True)
    return top + jnp.log(jnp.sum(jnp.exp(terms - top), axis=0, keepdims=True))


def combine(values, keys, key):
    return logsum(jnp.where(keys == key, values, NEG_BIG))


def in_turn(t, n):
    if isinstance(t, int):
        return (t + 1) // 2 % (n // 2) if t % 2 else n // 2 + t // 2
    return jnp.where(t % 2 == 0, n // 2 + t // 2, lax.rem((t + 1) // 2, n // 2))


def far_first(t, n):
    if isinstance(t, int):
        return (n // 2 + t) if t < n // 2 else (t - n // 2 + 1) % (n // 2)
    return jnp.where(t < n // 2, n // 2 + t, lax.rem(t - n // 2 + 1, n // 2))


def exchange_kernel(
    n, blocks, half, scale,
    pair_source, pair_target, pair_count, src_hbm, tgt_hbm,
    rx_out, ids_out, a_out, b_out, source_out, target_out,
    src, tgt, out_x, rx, score, score_t, b_col, want_rows, ids_in, ids_all, ids_smem, id_keys,
    source_pick, wanted, source_keys, stats_out, stats_in, stat_rows, rep_out, rep_in, a_src, a_send, a_in, a_rows, a_all, b_all,
    b_pad, x_sq, y_sq,
    load_sem, x_send, x_recv, id_send, id_recv, fwd_send, fwd_recv, keep_sem,
    stat_send, stat_recv, a_ssem, a_rsem, rep_send, rep_recv, tail_send, tail_recv,
):
    me = lax.axis_index("pts")
    side = lax.axis_index("rep")
    other = 1 - side
    first = side * half

    load_src = pltpu.make_async_copy(src_hbm, src, load_sem.at[0])
    load_tgt = pltpu.make_async_copy(tgt_hbm, tgt, load_sem.at[1])
    load_src.start()
    load_tgt.start()

    barrier = pltpu.get_barrier_semaphore()

    def greet(d):
        pl.semaphore_signal(
            barrier, inc=1, device_id=(lax.rem(me + d, n), side), device_id_type=MESH
        )

    loop(1, n, greet)
    pl.semaphore_signal(barrier, inc=1, device_id=(me, other), device_id_type=MESH)

    slots = pair_source.shape[0]
    count = pair_count[0]

    def list_row(p):
        def look(k, found):
            offset = pair_target[k] - p * blocks
            mine = (k < count) & (offset >= 0) & (offset < blocks)
            local_source = pair_source[k] - me * blocks
            return jnp.where(mine, local_source, found[0]), jnp.where(mine, offset, found[1])

        found = (jnp.int32(-1), jnp.int32(-1))
        if slots <= 16:
            for k in range(slots):
                found = look(k, found)
        else:
            found = lax.fori_loop(0, slots, look, found)
        source_pick[p], wanted[p] = found
        want_rows[p] = jnp.full((1, BLOCK), found[1], jnp.int32)
        source_keys[pl.ds(p, 1), :] = jnp.full((1, BLOCK), found[0], jnp.int32)

    loop(0, n, list_row)
    pl.semaphore_wait(barrier, n)

    def to_peer(src_ref, dst_ref, send_sem, recv_sem, peer):
        return pltpu.make_async_remote_copy(
            src_ref=src_ref, dst_ref=dst_ref, send_sem=send_sem, recv_sem=recv_sem,
            device_id=(peer, side), device_id_type=MESH,
        )

    def to_twin(src_ref, dst_ref, send_sem, recv_sem):
        return pltpu.make_async_remote_copy(
            src_ref=src_ref, dst_ref=dst_ref, send_sem=send_sem, recv_sem=recv_sem,
            device_id=(me, other), device_id_type=MESH,
        )

    def id_copy(peer, slot):
        return to_peer(want_rows.at[peer], ids_in.at[slot], id_send.at[peer], id_recv.at[slot], peer)

    def x_copy(peer, slot):
        return to_peer(out_x.at[peer], rx.at[slot], x_send.at[peer], x_recv.at[slot], peer)

    def stat_copy(it, peer, slot):
        return to_peer(
            stats_out.at[it, peer], stats_in.at[it, slot],
            stat_send.at[it], stat_recv.at[it], peer,
        )

    def stat_total(it):
        part = pl.ds(0, n - 1)
        return to_twin(
            stats_out.at[it, part], stats_in.at[it, part], stat_send.at[it], stat_recv.at[it]
        )

    def a_total(it):
        part = pl.ds(0, n - 1)
        return to_twin(a_send.at[it, part], a_in.at[it, part], a_ssem.at[it], a_rsem.at[it])

    def swap(it):
        return to_twin(rep_out.at[it], rep_in.at[it], rep_send.at[it], rep_recv.at[it])

    def a_copy(it, peer, slot):
        return to_peer(
            a_send.at[it, peer], a_in.at[it, slot], a_ssem.at[it], a_rsem.at[it], peer
        )

    def keep_copy(slot):
        return pltpu.make_async_copy(rx.at[slot], rx_out.at[side, slot], keep_sem.at[slot])

    def forward_copy(slot, which):
        return to_twin(
            rx.at[slot], rx_out.at[which, slot], fwd_send.at[slot], fwd_recv.at[slot]
        )

    def tail_copy(k, ref, which):
        return to_twin(ref.at[which], ref.at[which], tail_send.at[k], tail_recv.at[k])

    loop(1, n, lambda d: id_copy(lax.rem(me + d, n), me).start())
    load_src.wait()

    def send_block(d):
        peer = flipped(me, d, n)
        out_x[peer] = src[jnp.maximum(source_pick[peer], 0)]
        x_copy(peer, me).start()

    spread(0, n - 1, lambda t: send_block(in_turn(t, n)))
    rx[me] = src[jnp.maximum(source_pick[me], 0)]
    ids_in[me] = want_rows[me]
    load_tgt.wait()
    b_pad[...] = jnp.zeros(b_pad.shape, jnp.float32)

    def source_squares(b):
        x_sq[pl.ds(b, 1), :] = scale * square_row(src[b])

    def target_squares(b):
        row = scale * square_row(tgt[b])
        y_sq[pl.ds(b, 1), :] = row
        b_col[b] = as_column(-row)

    loop(0, blocks, source_squares)
    loop(0, blocks, target_squares)

    def take_id(d):
        peer = lax.rem(me + d, n)
        id_copy(peer, peer).wait_recv()

    loop(1, n, take_id)
    ids_move = pltpu.make_async_copy(ids_in, ids_smem, load_sem.at[2])
    ids_move.start()

    def id_row(q):
        row = ids_in[q]
        id_keys[pl.ds(q, 1), :] = row
        ids_all[side, pl.ds(q, 1), :] = row

    loop(0, n, id_row)
    tail_copy(0, ids_all, side).start()
    ids_move.wait()

    def local_id(q):
        return jnp.maximum(ids_smem[q, 0, 0], 0)

    def arrivals(group):
        offsets = [in_turn(group * 4 + k, n) for k in range(4)]
        peers = [flipped(me, d, n) for d in offsets]
        for d, peer in zip(offsets, peers):
            unless_zero(d, lambda peer=peer: x_copy(peer, peer).wait_recv())

        picks = [local_id(peer) for peer in peers]
        grids = [
            lax.dot_general(
                rx[peer], tgt[pick], (((1,), (1,)), ((), ())), preferred_element_type=jnp.float32
            ) * (2.0 * scale)
            for peer, pick in zip(peers, picks)
        ]
        turned = [jnp.transpose(grid) for grid in grids]
        rows = [logsum(b_col[pick] + grid_t) for pick, grid_t in zip(picks, turned)]
        for peer, row in zip(peers, rows):
            stats_out[0, peer] = row
        for d, peer in zip(offsets, peers):
            unless_zero(d, lambda peer=peer: stat_copy(0, peer, me).start())

        for peer, grid, grid_t in zip(peers, grids, turned):
            score[peer] = grid
            score_t[peer] = grid_t
        for peer in peers:
            keep_copy(peer).start()
            forward_copy(peer, side).start()

    spread(0, n // 4, arrivals)

    def finish_blocks(d):
        peer = lax.rem(me + d, n)
        id_copy(peer, me).wait_send()
        x_copy(peer, me).wait_send()

    def finish_forwards(q):
        keep_copy(q).wait()
        forward_copy(q, other).wait_recv()
        forward_copy(q, side).wait_send()

    for it in range(ITERS):
        if it == 1:
            loop(1, n, finish_blocks)
        if it == 2:
            loop(0, n, finish_forwards)
        if it > 0:
            stat_total(it - 1).wait_send()
            a_total(it - 1).wait_send()
            swap(it - 1).wait_send()
        stat_total(it).wait_recv()
        stats_in[it, me] = stats_out[it, me]

        def stat_row(p):
            stat_rows[pl.ds(p, 1), :] = stats_in[it, p]

        grouped(n, 8, stat_row)
        values, keys = stat_rows[...], source_keys[...]
        rows = [combine(values, keys, b) for b in range(blocks)]
        for b, row in enumerate(rows):
            rep_out[it, b:b + 1, :] = row
        swap(it).start()
        swap(it).wait_recv()
        top = jnp.maximum(rep_out[it], rep_in[it])
        total = jnp.exp(rep_out[it] - top) + jnp.exp(rep_in[it] - top)
        a_src[...] = -(top + jnp.log(total))

        def send_a(d):
            peer = lax.rem(me + far_first(d, n), n)
            a_send[it, peer] = a_src[pl.ds(jnp.maximum(source_pick[peer], 0), 1), :]
            a_copy(it, peer, me).start()

        spread(0, n - 1, send_a)
        a_in[it, me] = a_src[pl.ds(jnp.maximum(source_pick[me], 0), 1), :]

        a_total(it).wait_recv()

        def a_row(q):
            a_rows[pl.ds(q, 1), :] = a_in[it, q]

        grouped(n, 8, a_row)
        if it + 1 == ITERS:
            a_all[side] = a_rows[...]
            tail_copy(1, a_all, side).start()

        def column_visits(chunk):
            base = chunk * 16
            columns = columns_of(a_rows[pl.ds(pl.multiple_of(base, 16), 16), :])
            rows = [logsum(column + score[base + k]) for k, column in enumerate(columns)]
            for k, row in enumerate(rows):
                stat_rows[pl.ds(base + k, 1), :] = row

        loop(0, n // 16, column_visits)
        values, keys = stat_rows[...], id_keys[...]
        rows = [-combine(values, keys, b + first) for b in range(half)]
        for b, row in enumerate(rows):
            b_pad[b:b + 1, :] = row
        if it + 1 == ITERS:
            b_all[side] = b_pad[0:half, :]
        else:
            for b, column in enumerate(columns_of(b_pad[...])[:half]):
                b_col[first + b] = column

            def next_rows(group):
                offsets = [far_first(group * 8 + k, n) for k in range(8)]
                peers = [lax.rem(me + d, n) for d in offsets]
                rows = [logsum(b_col[local_id(q)] + score_t[q]) for q in peers]
                for q, row in zip(peers, rows):
                    stats_out[it + 1, q] = row
                for d, q in zip(offsets, peers):
                    unless_zero(d, lambda q=q: stat_copy(it + 1, q, me).start())

            spread(0, n // 8, next_rows)

    tail_copy(2, b_all, side).start()
    source_out[...] = EPSILON * (a_src[...] + x_sq[...])

    stat_total(ITERS - 1).wait_send()
    a_total(ITERS - 1).wait_send()
    swap(ITERS - 1).wait_send()
    for k, ref in enumerate((ids_all, a_all, b_all)):
        tail_copy(k, ref, other).wait_recv()
        tail_copy(k, ref, side).wait_send()
    ids_out[...] = ids_all[...]
    a_out[...] = a_all[...]
    for part in range(2):
        b_out[part * half:(part + 1) * half, :] = b_all[part]
    target_out[...] = EPSILON * (b_out[...] + y_sq[...])


def gradient_kernel(
    pairs, blocks, scale, ids, rx_hbm, a_rows, b_rows, tgt_hbm, source_in, target_in,
    out, source_out, target_out, rx, tgt, grad, b_col, mass, sems, out_sems,
):
    groups = pairs // 4

    def fetch(group):
        part = pl.ds(group * 4, 4)
        return pltpu.make_async_copy(rx_hbm.at[part], rx.at[part], sems.at[group])

    def store(b):
        return pltpu.make_async_copy(grad.at[b], out.at[b], out_sems.at[b])

    load_tgt = pltpu.make_async_copy(tgt_hbm, tgt, out_sems.at[blocks])
    load_tgt.start()
    loop(0, groups, lambda group: fetch(group).start())
    source_out[...] = source_in[...]
    target_out[...] = target_in[...]
    for b, column in enumerate(columns_of(b_rows[...])):
        b_col[b] = column

    def prepare(b):
        grad[b] = jnp.zeros(grad.shape[1:], jnp.float32)
        mass[b] = jnp.zeros((BLOCK, BLOCK), jnp.float32)

    grouped(blocks, 4, prepare)
    load_tgt.wait()

    def visit(group):
        fetch(group).wait()
        results = []
        for k in range(4):
            q = group * 4 + k
            target = ids[q, 0]
            pick = jnp.maximum(target, 0)
            grid = lax.dot_general(
                tgt[pick], rx[q], (((1,), (1,)), ((), ())), preferred_element_type=jnp.float32
            ) * (2.0 * scale)
            plan = jnp.exp(b_col[pick] + (grid + a_rows[pl.ds(q, 1), :]))
            plan = jnp.where(target >= 0, plan, 0.0)
            part = jnp.dot(plan.astype(jnp.bfloat16), rx[q], preferred_element_type=jnp.float32)
            results.append((pick, plan, part))
        for pick, plan, part in results:
            grad[pick] += part
            mass[pick] += plan

    loop(0, groups, visit)

    def finish(group):
        for k in range(4):
            b = group * 4 + k
            column = jnp.sum(mass[b], axis=1, keepdims=True)
            grad[b] = tgt[b].astype(jnp.float32) * column - grad[b]
        for k in range(4):
            store(group * 4 + k).start()

    loop(0, blocks // 4, finish)
    loop(0, blocks, lambda b: store(b).wait())


def on_device(src_points, tgt_points, pair_source, pair_target, pair_count):
    n = lax.axis_size("pts")
    reps = lax.axis_size("rep")
    rows, dim = src_points.shape
    blocks = rows // BLOCK
    half = blocks // reps
    scale = 1.0 / EPSILON / dim
    src = src_points.reshape(blocks, BLOCK, dim)
    tgt = tgt_points.reshape(blocks, BLOCK, dim)

    f32, bf16, i32 = jnp.float32, jnp.bfloat16, jnp.int32
    shape = jax.ShapeDtypeStruct
    vmem = pl.BlockSpec(memory_space=pltpu.VMEM)
    smem = pl.BlockSpec(memory_space=pltpu.SMEM)
    hbm = pl.BlockSpec(memory_space=pl.ANY)
    dma = pltpu.SemaphoreType.DMA
    with jax.named_scope("exchange_and_sweeps"):
        rx, ids, a_rows, b_rows, source_dual, target_dual = pl.pallas_call(
            functools.partial(exchange_kernel, n, blocks, half, scale),
            out_shape=(
                shape((reps, n, BLOCK, dim), bf16),
                shape((reps, n, BLOCK), i32),
                shape((reps, n, BLOCK), f32),
                shape((blocks, BLOCK), f32),
                shape((blocks, BLOCK), f32),
                shape((blocks, BLOCK), f32),
            ),
            in_specs=[smem, smem, smem, hbm, hbm],
            out_specs=(hbm, vmem, vmem, vmem, vmem, vmem),
            scratch_shapes=[
                pltpu.VMEM((blocks, BLOCK, dim), bf16),
                pltpu.VMEM((blocks, BLOCK, dim), bf16),
                pltpu.VMEM((n, BLOCK, dim), bf16),
                pltpu.VMEM((n, BLOCK, dim), bf16),
                pltpu.VMEM((n, BLOCK, BLOCK), f32),
                pltpu.VMEM((n, BLOCK, BLOCK), f32),
                pltpu.VMEM((blocks, BLOCK, BLOCK), f32),
                pltpu.VMEM((n, 1, BLOCK), i32),
                pltpu.VMEM((n, 1, BLOCK), i32),
                pltpu.VMEM((reps, n, BLOCK), i32),
                pltpu.SMEM((n, 1, BLOCK), i32),
                pltpu.VMEM((n, BLOCK), i32),
                pltpu.SMEM((n,), i32),
                pltpu.SMEM((n,), i32),
                pltpu.VMEM((n, BLOCK), i32),
                pltpu.VMEM((ITERS, n, 1, BLOCK), f32),
                pltpu.VMEM((ITERS, n, 1, BLOCK), f32),
                pltpu.VMEM((n, BLOCK), f32),
                pltpu.VMEM((ITERS, blocks, BLOCK), f32),
                pltpu.VMEM((ITERS, blocks, BLOCK), f32),
                pltpu.VMEM((blocks, BLOCK), f32),
                pltpu.VMEM((ITERS, n, 1, BLOCK), f32),
                pltpu.VMEM((ITERS, n, 1, BLOCK), f32),
                pltpu.VMEM((n, BLOCK), f32),
                pltpu.VMEM((reps, n, BLOCK), f32),
                pltpu.VMEM((reps, half, BLOCK), f32),
                pltpu.VMEM((-(-half // 8) * 8, BLOCK), f32),
                pltpu.VMEM((blocks, BLOCK), f32),
                pltpu.VMEM((blocks, BLOCK), f32),
                dma((3,)),
                dma((n,)), dma((n,)), dma((n,)), dma((n,)), dma((n,)), dma((n,)), dma((n,)),
                dma((ITERS,)), dma((ITERS,)), dma((ITERS,)), dma((ITERS,)),
                dma((ITERS,)), dma((ITERS,)), dma((3,)), dma((3,)),
            ],
            compiler_params=pltpu.CompilerParams(
                collective_id=0, has_side_effects=True, vmem_limit_bytes=VMEM_BYTES
            ),
            name="exchange_and_sweeps",
        )(pair_source, pair_target, pair_count, src, tgt)
    pairs = reps * n
    with jax.named_scope("gradient"):
        grad, source_dual, target_dual = pl.pallas_call(
            functools.partial(gradient_kernel, pairs, blocks, scale),
            out_shape=(
                shape((blocks, BLOCK, dim), f32),
                shape((blocks, BLOCK), f32),
                shape((blocks, BLOCK), f32),
            ),
            in_specs=[smem, hbm, vmem, vmem, hbm, vmem, vmem],
            out_specs=(hbm, vmem, vmem),
            scratch_shapes=[
                pltpu.VMEM((pairs, BLOCK, dim), bf16),
                pltpu.VMEM((blocks, BLOCK, dim), bf16),
                pltpu.VMEM((blocks, BLOCK, dim), f32),
                pltpu.VMEM((blocks, BLOCK, BLOCK), f32),
                pltpu.VMEM((blocks, BLOCK, BLOCK), f32),
                dma((pairs // 4,)),
                dma((blocks + 1,)),
            ],
            compiler_params=pltpu.CompilerParams(vmem_limit_bytes=VMEM_BYTES),
            name="gradient",
        )(
            ids.reshape(pairs, BLOCK),
            rx.reshape(pairs, BLOCK, dim),
            a_rows.reshape(pairs, BLOCK),
            b_rows,
            tgt,
            source_dual,
            target_dual,
        )
    return source_dual.reshape(-1), target_dual.reshape(-1), grad.reshape(rows, dim)


def solution(mesh):
    return jax.shard_map(
        on_device,
        mesh=mesh,
        in_specs=(
            P("pts", None),
            P("pts", None),
            P(("pts", "rep")),
            P(("pts", "rep")),
            P(("pts", "rep")),
        ),
        out_specs=(P("pts"), P("pts"), P("pts", None)),
        check_vma=False,
    )
```

```python
import functools

import jax
import jax.numpy as jnp
from jax import lax
from jax.experimental import pallas as pl
from jax.experimental.pallas import tpu as pltpu
from jax.sharding import PartitionSpec as P

BLOCK = 128
ITERS = 3
EPSILON = 0.05
NEG_BIG = -1e30
MESH = pl.DeviceIdType.MESH
VMEM_BYTES = 56 * 1024 * 1024


def loop(lower, upper, body):
    def step(i, carry):
        body(i)
        return carry

    lax.fori_loop(lower, upper, step, 0)


def spread(lower, upper, body):
    if upper - lower <= 16:
        for i in range(lower, upper):
            body(i)
    else:
        loop(lower, upper, body)


def unless_zero(d, action):
    if not isinstance(d, int):
        pl.when(d > 0)(action)
    elif d:
        action()


def grouped(total, size, body):
    def step(i):
        for k in range(size):
            body(i * size + k)

    loop(0, total // size, step)


def flipped(me, d, n):
    if n & (n - 1):
        return lax.rem(me + d, n)
    out, bit = 0, 1
    while bit < n:
        out = out + bit * (((me // bit) + (d // bit)) % 2)
        bit *= 2
    return out


def columns_of(rows):
    turned = jnp.transpose(rows)
    return [jnp.broadcast_to(turned[:, k:k + 1], (BLOCK, BLOCK)) for k in range(rows.shape[0])]


def square_row(block):
    values = block.astype(jnp.float32)
    squares = values * values
    high = squares.astype(jnp.bfloat16)
    low = (squares - high.astype(jnp.float32)).astype(jnp.bfloat16)
    ones = jnp.ones((8, block.shape[1]), jnp.bfloat16)
    along = (((1,), (1,)), ((), ()))
    total = lax.dot_general(ones, high, along, preferred_element_type=jnp.float32)
    total += lax.dot_general(ones, low, along, preferred_element_type=jnp.float32)
    return total[0:1, :]


def logsum(terms):
    top = jnp.max(terms, axis=0, keepdims=True)
    return top + jnp.log(jnp.sum(jnp.exp(terms - top), axis=0, keepdims=True))


def combine(values, keys, key):
    return logsum(jnp.where(keys == key, values, NEG_BIG))


def in_turn(t, n):
    if isinstance(t, int):
        return (t + 1) // 2 % (n // 2) if t % 2 else n // 2 + t // 2
    return jnp.where(t % 2 == 0, n // 2 + t // 2, lax.rem((t + 1) // 2, n // 2))


def far_first(t, n):
    if isinstance(t, int):
        return (n // 2 + t) if t < n // 2 else (t - n // 2 + 1) % (n // 2)
    return jnp.where(t < n // 2, n // 2 + t, lax.rem(t - n // 2 + 1, n // 2))


def exchange_kernel(
    n, blocks, half, scale,
    pair_source, pair_target, pair_count, src_hbm, tgt_hbm,
    rx_out, ids_out, a_out, b_out, source_out, target_out,
    src, tgt, out_x, rx, score, score_t, b_col, want_rows, ids_in, ids_all, ids_smem, id_keys,
    source_pick, wanted, source_keys, stats_out, stats_in, stat_rows, rep_out, rep_in, a_src, a_send, a_in, a_rows, a_all, b_all,
    b_pad, x_sq, y_sq,
    load_sem, x_send, x_recv, id_send, id_recv, fwd_send, fwd_recv, keep_sem,
    stat_send, stat_recv, a_ssem, a_rsem, rep_send, rep_recv, tail_send, tail_recv,
):
    me = lax.axis_index("pts")
    side = lax.axis_index("rep")
    other = 1 - side
    first = side * half

    load_src = pltpu.make_async_copy(src_hbm, src, load_sem.at[0])
    load_tgt = pltpu.make_async_copy(tgt_hbm, tgt, load_sem.at[1])
    load_src.start()
    load_tgt.start()

    barrier = pltpu.get_barrier_semaphore()

    def greet(d):
        pl.semaphore_signal(
            barrier, inc=1, device_id=(lax.rem(me + d, n), side), device_id_type=MESH
        )

    loop(1, n, greet)
    pl.semaphore_signal(barrier, inc=1, device_id=(me, other), device_id_type=MESH)

    slots = pair_source.shape[0]
    count = pair_count[0]

    def list_row(p):
        def look(k, found):
            offset = pair_target[k] - p * blocks
            mine = (k < count) & (offset >= 0) & (offset < blocks)
            local_source = pair_source[k] - me * blocks
            return jnp.where(mine, local_source, found[0]), jnp.where(mine, offset, found[1])

        found = (jnp.int32(-1), jnp.int32(-1))
        if slots <= 16:
            for k in range(slots):
                found = look(k, found)
        else:
            found = lax.fori_loop(0, slots, look, found)
        source_pick[p], wanted[p] = found
        want_rows[p] = jnp.full((1, BLOCK), found[1], jnp.int32)
        source_keys[pl.ds(p, 1), :] = jnp.full((1, BLOCK), found[0], jnp.int32)

    loop(0, n, list_row)
    pl.semaphore_wait(barrier, n)

    def to_peer(src_ref, dst_ref, send_sem, recv_sem, peer):
        return pltpu.make_async_remote_copy(
            src_ref=src_ref, dst_ref=dst_ref, send_sem=send_sem, recv_sem=recv_sem,
            device_id=(peer, side), device_id_type=MESH,
        )

    def to_twin(src_ref, dst_ref, send_sem, recv_sem):
        return pltpu.make_async_remote_copy(
            src_ref=src_ref, dst_ref=dst_ref, send_sem=send_sem, recv_sem=recv_sem,
            device_id=(me, other), device_id_type=MESH,
        )

    def id_copy(peer, slot):
        return to_peer(want_rows.at[peer], ids_in.at[slot], id_send.at[peer], id_recv.at[slot], peer)

    def x_copy(peer, slot):
        return to_peer(out_x.at[peer], rx.at[slot], x_send.at[peer], x_recv.at[slot], peer)

    def stat_copy(it, peer, slot):
        return to_peer(
            stats_out.at[it, peer], stats_in.at[it, slot],
            stat_send.at[it], stat_recv.at[it], peer,
        )

    def stat_total(it):
        part = pl.ds(0, n - 1)
        return to_twin(
            stats_out.at[it, part], stats_in.at[it, part], stat_send.at[it], stat_recv.at[it]
        )

    def a_total(it):
        part = pl.ds(0, n - 1)
        return to_twin(a_send.at[it, part], a_in.at[it, part], a_ssem.at[it], a_rsem.at[it])

    def swap(it):
        return to_twin(rep_out.at[it], rep_in.at[it], rep_send.at[it], rep_recv.at[it])

    def a_copy(it, peer, slot):
        return to_peer(
            a_send.at[it, peer], a_in.at[it, slot], a_ssem.at[it], a_rsem.at[it], peer
        )

    def keep_copy(slot):
        return pltpu.make_async_copy(rx.at[slot], rx_out.at[side, slot], keep_sem.at[slot])

    def forward_copy(slot, which):
        return to_twin(
            rx.at[slot], rx_out.at[which, slot], fwd_send.at[slot], fwd_recv.at[slot]
        )

    def tail_copy(k, ref, which):
        return to_twin(ref.at[which], ref.at[which], tail_send.at[k], tail_recv.at[k])

    loop(1, n, lambda d: id_copy(lax.rem(me + d, n), me).start())
    load_src.wait()

    def send_block(d):
        peer = flipped(me, d, n)
        out_x[peer] = src[jnp.maximum(source_pick[peer], 0)]
        x_copy(peer, me).start()

    spread(0, n - 1, lambda t: send_block(in_turn(t, n)))
    rx[me] = src[jnp.maximum(source_pick[me], 0)]
    ids_in[me] = want_rows[me]
    load_tgt.wait()
    b_pad[...] = jnp.zeros(b_pad.shape, jnp.float32)

    def source_squares(b):
        x_sq[pl.ds(b, 1), :] = scale * square_row(src[b])

    def target_squares(b):
        y_sq[pl.ds(b, 1), :] = scale * square_row(tgt[b])

    grouped(blocks, 4, target_squares)
    grouped(blocks, 4, source_squares)
    for b, column in enumerate(columns_of(y_sq[...])):
        b_col[b] = -column

    def take_id(d):
        peer = lax.rem(me + d, n)
        id_copy(peer, peer).wait_recv()

    loop(1, n, take_id)
    ids_move = pltpu.make_async_copy(ids_in, ids_smem, load_sem.at[2])
    ids_move.start()

    def id_row(q):
        row = ids_in[q]
        id_keys[pl.ds(q, 1), :] = row
        ids_all[side, pl.ds(q, 1), :] = row

    loop(0, n, id_row)
    tail_copy(0, ids_all, side).start()
    ids_move.wait()

    def local_id(q):
        return jnp.maximum(ids_smem[q, 0, 0], 0)

    def arrivals(group):
        offsets = [in_turn(group * 4 + k, n) for k in range(4)]
        peers = [flipped(me, d, n) for d in offsets]
        for d, peer in zip(offsets, peers):
            unless_zero(d, lambda peer=peer: x_copy(peer, peer).wait_recv())

        picks = [local_id(peer) for peer in peers]
        grids = [
            lax.dot_general(
                rx[peer], tgt[pick], (((1,), (1,)), ((), ())), preferred_element_type=jnp.float32
            ) * (2.0 * scale)
            for peer, pick in zip(peers, picks)
        ]
        turned = [jnp.transpose(grid) for grid in grids]
        rows = [logsum(b_col[pick] + grid_t) for pick, grid_t in zip(picks, turned)]
        for peer, row in zip(peers, rows):
            stats_out[0, peer] = row
        for d, peer in zip(offsets, peers):
            unless_zero(d, lambda peer=peer: stat_copy(0, peer, me).start())

        for peer, grid, grid_t in zip(peers, grids, turned):
            score[peer] = grid
            score_t[peer] = grid_t
        for peer in peers:
            keep_copy(peer).start()
            forward_copy(peer, side).start()

    spread(0, n // 4, arrivals)

    def finish_blocks(d):
        peer = lax.rem(me + d, n)
        id_copy(peer, me).wait_send()
        x_copy(peer, me).wait_send()

    def finish_forwards(q):
        keep_copy(q).wait()
        forward_copy(q, other).wait_recv()
        forward_copy(q, side).wait_send()

    for it in range(ITERS):
        if it == 1:
            loop(1, n, finish_blocks)
        if it == 2:
            loop(0, n, finish_forwards)
        if it > 0:
            stat_total(it - 1).wait_send()
            a_total(it - 1).wait_send()
            swap(it - 1).wait_send()
        stat_total(it).wait_recv()
        stats_in[it, me] = stats_out[it, me]

        def stat_row(p):
            stat_rows[pl.ds(p, 1), :] = stats_in[it, p]

        grouped(n, 8, stat_row)
        values, keys = stat_rows[...], source_keys[...]
        rows = [combine(values, keys, b) for b in range(blocks)]
        for b, row in enumerate(rows):
            rep_out[it, b:b + 1, :] = row
        swap(it).start()
        swap(it).wait_recv()
        top = jnp.maximum(rep_out[it], rep_in[it])
        total = jnp.exp(rep_out[it] - top) + jnp.exp(rep_in[it] - top)
        a_src[...] = -(top + jnp.log(total))

        def send_a(d):
            peer = lax.rem(me + far_first(d, n), n)
            a_send[it, peer] = a_src[pl.ds(jnp.maximum(source_pick[peer], 0), 1), :]
            a_copy(it, peer, me).start()

        spread(0, n - 1, send_a)
        a_in[it, me] = a_src[pl.ds(jnp.maximum(source_pick[me], 0), 1), :]

        a_total(it).wait_recv()

        def a_row(q):
            a_rows[pl.ds(q, 1), :] = a_in[it, q]

        grouped(n, 8, a_row)
        if it + 1 == ITERS:
            a_all[side] = a_rows[...]
            tail_copy(1, a_all, side).start()

        def column_visits(chunk):
            base = chunk * 16
            columns = columns_of(a_rows[pl.ds(pl.multiple_of(base, 16), 16), :])
            rows = [logsum(column + score[base + k]) for k, column in enumerate(columns)]
            for k, row in enumerate(rows):
                stat_rows[pl.ds(base + k, 1), :] = row

        loop(0, n // 16, column_visits)
        values, keys = stat_rows[...], id_keys[...]
        rows = [-combine(values, keys, b + first) for b in range(half)]
        for b, row in enumerate(rows):
            b_pad[b:b + 1, :] = row
        if it + 1 == ITERS:
            b_all[side] = b_pad[0:half, :]
        else:
            for b, column in enumerate(columns_of(b_pad[...])[:half]):
                b_col[first + b] = column

            def next_rows(group):
                offsets = [far_first(group * 8 + k, n) for k in range(8)]
                peers = [lax.rem(me + d, n) for d in offsets]
                rows = [logsum(b_col[local_id(q)] + score_t[q]) for q in peers]
                for q, row in zip(peers, rows):
                    stats_out[it + 1, q] = row
                for d, q in zip(offsets, peers):
                    unless_zero(d, lambda q=q: stat_copy(it + 1, q, me).start())

            spread(0, n // 8, next_rows)

    tail_copy(2, b_all, side).start()
    source_out[...] = EPSILON * (a_src[...] + x_sq[...])

    stat_total(ITERS - 1).wait_send()
    a_total(ITERS - 1).wait_send()
    swap(ITERS - 1).wait_send()
    for k, ref in enumerate((ids_all, a_all, b_all)):
        tail_copy(k, ref, other).wait_recv()
        tail_copy(k, ref, side).wait_send()
    ids_out[...] = ids_all[...]
    a_out[...] = a_all[...]
    for part in range(2):
        b_out[part * half:(part + 1) * half, :] = b_all[part]
    target_out[...] = EPSILON * (b_out[...] + y_sq[...])


def gradient_kernel(
    pairs, blocks, scale, ids, rx_hbm, a_rows, b_rows, tgt_hbm, source_in, target_in,
    out, source_out, target_out, rx, tgt, grad, b_col, mass, sems, out_sems,
):
    groups = pairs // 8

    def fetch(group):
        part = pl.ds(group * 8, 8)
        return pltpu.make_async_copy(rx_hbm.at[part], rx.at[part], sems.at[group])

    def store(b):
        return pltpu.make_async_copy(grad.at[b], out.at[b], out_sems.at[b])

    load_tgt = pltpu.make_async_copy(tgt_hbm, tgt, out_sems.at[blocks])
    load_tgt.start()
    loop(0, groups, lambda group: fetch(group).start())
    source_out[...] = source_in[...]
    target_out[...] = target_in[...]
    for b, column in enumerate(columns_of(b_rows[...])):
        b_col[b] = column

    def prepare(b):
        grad[b] = jnp.zeros(grad.shape[1:], jnp.float32)
        mass[b] = jnp.zeros((BLOCK, BLOCK), jnp.float32)

    grouped(blocks, 4, prepare)
    load_tgt.wait()

    def visit(group):
        fetch(group).wait()
        results = []
        for k in range(8):
            q = group * 8 + k
            target = ids[q, 0]
            pick = jnp.maximum(target, 0)
            grid = lax.dot_general(
                tgt[pick], rx[q], (((1,), (1,)), ((), ())), preferred_element_type=jnp.float32
            ) * (2.0 * scale)
            plan = jnp.exp(b_col[pick] + (grid + a_rows[pl.ds(q, 1), :]))
            plan = jnp.where(target >= 0, plan, 0.0)
            part = jnp.dot(plan.astype(jnp.bfloat16), rx[q], preferred_element_type=jnp.float32)
            results.append((pick, plan, part))
        for pick, plan, part in results:
            grad[pick] += part
            mass[pick] += plan

    loop(0, groups, visit)

    def finish(group):
        for k in range(4):
            b = group * 4 + k
            column = jnp.sum(mass[b], axis=1, keepdims=True)
            grad[b] = tgt[b].astype(jnp.float32) * column - grad[b]
        for k in range(4):
            store(group * 4 + k).start()

    loop(0, blocks // 4, finish)
    loop(0, blocks, lambda b: store(b).wait())


def on_device(src_points, tgt_points, pair_source, pair_target, pair_count):
    n = lax.axis_size("pts")
    reps = lax.axis_size("rep")
    rows, dim = src_points.shape
    blocks = rows // BLOCK
    half = blocks // reps
    scale = 1.0 / EPSILON / dim
    src = src_points.reshape(blocks, BLOCK, dim)
    tgt = tgt_points.reshape(blocks, BLOCK, dim)

    f32, bf16, i32 = jnp.float32, jnp.bfloat16, jnp.int32
    shape = jax.ShapeDtypeStruct
    vmem = pl.BlockSpec(memory_space=pltpu.VMEM)
    smem = pl.BlockSpec(memory_space=pltpu.SMEM)
    hbm = pl.BlockSpec(memory_space=pl.ANY)
    dma = pltpu.SemaphoreType.DMA
    with jax.named_scope("exchange_and_sweeps"):
        rx, ids, a_rows, b_rows, source_dual, target_dual = pl.pallas_call(
            functools.partial(exchange_kernel, n, blocks, half, scale),
            out_shape=(
                shape((reps, n, BLOCK, dim), bf16),
                shape((reps, n, BLOCK), i32),
                shape((reps, n, BLOCK), f32),
                shape((blocks, BLOCK), f32),
                shape((blocks, BLOCK), f32),
                shape((blocks, BLOCK), f32),
            ),
            in_specs=[smem, smem, smem, hbm, hbm],
            out_specs=(hbm, vmem, vmem, vmem, vmem, vmem),
            scratch_shapes=[
                pltpu.VMEM((blocks, BLOCK, dim), bf16),
                pltpu.VMEM((blocks, BLOCK, dim), bf16),
                pltpu.VMEM((n, BLOCK, dim), bf16),
                pltpu.VMEM((n, BLOCK, dim), bf16),
                pltpu.VMEM((n, BLOCK, BLOCK), f32),
                pltpu.VMEM((n, BLOCK, BLOCK), f32),
                pltpu.VMEM((blocks, BLOCK, BLOCK), f32),
                pltpu.VMEM((n, 1, BLOCK), i32),
                pltpu.VMEM((n, 1, BLOCK), i32),
                pltpu.VMEM((reps, n, BLOCK), i32),
                pltpu.SMEM((n, 1, BLOCK), i32),
                pltpu.VMEM((n, BLOCK), i32),
                pltpu.SMEM((n,), i32),
                pltpu.SMEM((n,), i32),
                pltpu.VMEM((n, BLOCK), i32),
                pltpu.VMEM((ITERS, n, 1, BLOCK), f32),
                pltpu.VMEM((ITERS, n, 1, BLOCK), f32),
                pltpu.VMEM((n, BLOCK), f32),
                pltpu.VMEM((ITERS, blocks, BLOCK), f32),
                pltpu.VMEM((ITERS, blocks, BLOCK), f32),
                pltpu.VMEM((blocks, BLOCK), f32),
                pltpu.VMEM((ITERS, n, 1, BLOCK), f32),
                pltpu.VMEM((ITERS, n, 1, BLOCK), f32),
                pltpu.VMEM((n, BLOCK), f32),
                pltpu.VMEM((reps, n, BLOCK), f32),
                pltpu.VMEM((reps, half, BLOCK), f32),
                pltpu.VMEM((-(-half // 8) * 8, BLOCK), f32),
                pltpu.VMEM((blocks, BLOCK), f32),
                pltpu.VMEM((blocks, BLOCK), f32),
                dma((3,)),
                dma((n,)), dma((n,)), dma((n,)), dma((n,)), dma((n,)), dma((n,)), dma((n,)),
                dma((ITERS,)), dma((ITERS,)), dma((ITERS,)), dma((ITERS,)),
                dma((ITERS,)), dma((ITERS,)), dma((3,)), dma((3,)),
            ],
            compiler_params=pltpu.CompilerParams(
                collective_id=0, has_side_effects=True, vmem_limit_bytes=VMEM_BYTES
            ),
            name="exchange_and_sweeps",
        )(pair_source, pair_target, pair_count, src, tgt)
    pairs = reps * n
    with jax.named_scope("gradient"):
        grad, source_dual, target_dual = pl.pallas_call(
            functools.partial(gradient_kernel, pairs, blocks, scale),
            out_shape=(
                shape((blocks, BLOCK, dim), f32),
                shape((blocks, BLOCK), f32),
                shape((blocks, BLOCK), f32),
            ),
            in_specs=[smem, hbm, vmem, vmem, hbm, vmem, vmem],
            out_specs=(hbm, vmem, vmem),
            scratch_shapes=[
                pltpu.VMEM((pairs, BLOCK, dim), bf16),
                pltpu.VMEM((blocks, BLOCK, dim), bf16),
                pltpu.VMEM((blocks, BLOCK, dim), f32),
                pltpu.VMEM((blocks, BLOCK, BLOCK), f32),
                pltpu.VMEM((blocks, BLOCK, BLOCK), f32),
                dma((pairs // 8,)),
                dma((blocks + 1,)),
            ],
            compiler_params=pltpu.CompilerParams(vmem_limit_bytes=VMEM_BYTES),
            name="gradient",
        )(
            ids.reshape(pairs, BLOCK),
            rx.reshape(pairs, BLOCK, dim),
            a_rows.reshape(pairs, BLOCK),
            b_rows,
            tgt,
            source_dual,
            target_dual,
        )
    return source_dual.reshape(-1), target_dual.reshape(-1), grad.reshape(rows, dim)


def solution(mesh):
    return jax.shard_map(
        on_device,
        mesh=mesh,
        in_specs=(
            P("pts", None),
            P("pts", None),
            P(("pts", "rep")),
            P(("pts", "rep")),
            P(("pts", "rep")),
        ),
        out_specs=(P("pts"), P("pts"), P("pts", None)),
        check_vma=False,
    )
```

```python
import functools

import jax
import jax.numpy as jnp
from jax import lax
from jax.experimental import pallas as pl
from jax.experimental.pallas import tpu as pltpu
from jax.sharding import PartitionSpec as P

BLOCK = 128
ITERS = 3
EPSILON = 0.05
NEG_BIG = -1e30
MESH = pl.DeviceIdType.MESH
VMEM_BYTES = 56 * 1024 * 1024


def loop(lower, upper, body):
    def step(i, carry):
        body(i)
        return carry

    lax.fori_loop(lower, upper, step, 0)


def spread(lower, upper, body):
    if upper - lower <= 16:
        for i in range(lower, upper):
            body(i)
    else:
        loop(lower, upper, body)


def unless_zero(d, action):
    if not isinstance(d, int):
        pl.when(d > 0)(action)
    elif d:
        action()


def grouped(total, size, body):
    def step(i):
        for k in range(size):
            body(i * size + k)

    loop(0, total // size, step)


def flipped(me, d, n):
    if n & (n - 1):
        return lax.rem(me + d, n)
    out, bit = 0, 1
    while bit < n:
        out = out + bit * (((me // bit) + (d // bit)) % 2)
        bit *= 2
    return out


def columns_of(rows):
    turned = jnp.transpose(rows)
    return [jnp.broadcast_to(turned[:, k:k + 1], (BLOCK, BLOCK)) for k in range(rows.shape[0])]


def square_row(block):
    values = block.astype(jnp.float32)
    squares = values * values
    high = squares.astype(jnp.bfloat16)
    low = (squares - high.astype(jnp.float32)).astype(jnp.bfloat16)
    ones = jnp.ones((8, block.shape[1]), jnp.bfloat16)
    along = (((1,), (1,)), ((), ()))
    total = lax.dot_general(ones, high, along, preferred_element_type=jnp.float32)
    total += lax.dot_general(ones, low, along, preferred_element_type=jnp.float32)
    return total[0:1, :]


def logsum(terms):
    top = jnp.max(terms, axis=0, keepdims=True)
    return top + jnp.log(jnp.sum(jnp.exp(terms - top), axis=0, keepdims=True))


def combine(values, keys, key):
    return logsum(jnp.where(keys == key, values, NEG_BIG))


def in_turn(t, n):
    if isinstance(t, int):
        return (t + 1) // 2 % (n // 2) if t % 2 else n // 2 + t // 2
    return jnp.where(t % 2 == 0, n // 2 + t // 2, lax.rem((t + 1) // 2, n // 2))


def far_first(t, n):
    if isinstance(t, int):
        return (n // 2 + t) if t < n // 2 else (t - n // 2 + 1) % (n // 2)
    return jnp.where(t < n // 2, n // 2 + t, lax.rem(t - n // 2 + 1, n // 2))


def exchange_kernel(
    n, blocks, half, scale,
    pair_source, pair_target, pair_count, src_hbm, tgt_hbm,
    rx_out, ids_out, a_out, b_out, source_out, target_out,
    src, tgt, out_x, rx, score, score_t, b_col, want_rows, ids_in, ids_all, ids_smem, id_keys,
    source_pick, wanted, source_keys, stats_out, stats_in, stat_rows, rep_out, rep_in, a_src, a_send, a_in, a_rows, a_all, b_all,
    b_pad, x_sq, y_sq,
    load_sem, x_send, x_recv, id_send, id_recv, fwd_send, fwd_recv, keep_sem,
    stat_send, stat_recv, a_ssem, a_rsem, rep_send, rep_recv, tail_send, tail_recv,
):
    me = lax.axis_index("pts")
    side = lax.axis_index("rep")
    other = 1 - side
    first = side * half

    load_src = pltpu.make_async_copy(src_hbm, src, load_sem.at[0])
    load_tgt = pltpu.make_async_copy(tgt_hbm, tgt, load_sem.at[1])
    load_src.start()
    load_tgt.start()

    barrier = pltpu.get_barrier_semaphore()

    def greet(d):
        pl.semaphore_signal(
            barrier, inc=1, device_id=(lax.rem(me + d, n), side), device_id_type=MESH
        )

    loop(1, n, greet)
    pl.semaphore_signal(barrier, inc=1, device_id=(me, other), device_id_type=MESH)

    slots = pair_source.shape[0]
    count = pair_count[0]

    def list_row(p):
        def look(k, found):
            offset = pair_target[k] - p * blocks
            mine = (k < count) & (offset >= 0) & (offset < blocks)
            local_source = pair_source[k] - me * blocks
            return jnp.where(mine, local_source, found[0]), jnp.where(mine, offset, found[1])

        found = (jnp.int32(-1), jnp.int32(-1))
        if slots <= 16:
            for k in range(slots):
                found = look(k, found)
        else:
            found = lax.fori_loop(0, slots, look, found)
        source_pick[p], wanted[p] = found
        want_rows[p] = jnp.full((1, BLOCK), found[1], jnp.int32)
        source_keys[pl.ds(p, 1), :] = jnp.full((1, BLOCK), found[0], jnp.int32)

    loop(0, n, list_row)
    pl.semaphore_wait(barrier, n)

    def to_peer(src_ref, dst_ref, send_sem, recv_sem, peer):
        return pltpu.make_async_remote_copy(
            src_ref=src_ref, dst_ref=dst_ref, send_sem=send_sem, recv_sem=recv_sem,
            device_id=(peer, side), device_id_type=MESH,
        )

    def to_twin(src_ref, dst_ref, send_sem, recv_sem):
        return pltpu.make_async_remote_copy(
            src_ref=src_ref, dst_ref=dst_ref, send_sem=send_sem, recv_sem=recv_sem,
            device_id=(me, other), device_id_type=MESH,
        )

    def id_copy(peer, slot):
        return to_peer(want_rows.at[peer], ids_in.at[slot], id_send.at[peer], id_recv.at[slot], peer)

    def x_copy(peer, slot):
        return to_peer(out_x.at[peer], rx.at[slot], x_send.at[peer], x_recv.at[slot], peer)

    def stat_copy(it, peer, slot):
        return to_peer(
            stats_out.at[it, peer], stats_in.at[it, slot],
            stat_send.at[it], stat_recv.at[it], peer,
        )

    def stat_total(it):
        part = pl.ds(0, n - 1)
        return to_twin(
            stats_out.at[it, part], stats_in.at[it, part], stat_send.at[it], stat_recv.at[it]
        )

    def a_total(it):
        part = pl.ds(0, n - 1)
        return to_twin(a_send.at[it, part], a_in.at[it, part], a_ssem.at[it], a_rsem.at[it])

    def swap(it):
        return to_twin(rep_out.at[it], rep_in.at[it], rep_send.at[it], rep_recv.at[it])

    def a_copy(it, peer, slot):
        return to_peer(
            a_send.at[it, peer], a_in.at[it, slot], a_ssem.at[it], a_rsem.at[it], peer
        )

    def keep_copy(slot):
        return pltpu.make_async_copy(rx.at[slot], rx_out.at[side, slot], keep_sem.at[slot])

    def forward_copy(slot, which):
        return to_twin(
            rx.at[slot], rx_out.at[which, slot], fwd_send.at[slot], fwd_recv.at[slot]
        )

    def tail_copy(k, ref, which):
        return to_twin(ref.at[which], ref.at[which], tail_send.at[k], tail_recv.at[k])

    loop(1, n, lambda d: id_copy(lax.rem(me + d, n), me).start())
    load_src.wait()

    def send_block(d):
        peer = flipped(me, d, n)
        out_x[peer] = src[jnp.maximum(source_pick[peer], 0)]
        x_copy(peer, me).start()

    spread(0, n - 1, lambda t: send_block(in_turn(t, n)))
    rx[me] = src[jnp.maximum(source_pick[me], 0)]
    ids_in[me] = want_rows[me]
    load_tgt.wait()
    b_pad[...] = jnp.zeros(b_pad.shape, jnp.float32)

    def source_squares(b):
        x_sq[pl.ds(b, 1), :] = scale * square_row(src[b])

    def target_squares(b):
        y_sq[pl.ds(b, 1), :] = scale * square_row(tgt[b])

    grouped(blocks, 4, target_squares)
    grouped(blocks, 4, source_squares)
    for b, column in enumerate(columns_of(y_sq[...])):
        b_col[b] = -column

    def take_id(d):
        peer = lax.rem(me + d, n)
        id_copy(peer, peer).wait_recv()

    loop(1, n, take_id)
    ids_move = pltpu.make_async_copy(ids_in, ids_smem, load_sem.at[2])
    ids_move.start()

    def id_row(q):
        row = ids_in[q]
        id_keys[pl.ds(q, 1), :] = row
        ids_all[side, pl.ds(q, 1), :] = row

    loop(0, n, id_row)
    tail_copy(0, ids_all, side).start()
    ids_move.wait()

    def local_id(q):
        return jnp.maximum(ids_smem[q, 0, 0], 0)

    def arrivals(group):
        offsets = [in_turn(group * 4 + k, n) for k in range(4)]
        peers = [flipped(me, d, n) for d in offsets]
        for d, peer in zip(offsets, peers):
            unless_zero(d, lambda peer=peer: x_copy(peer, peer).wait_recv())

        picks = [local_id(peer) for peer in peers]
        grids = [
            lax.dot_general(
                rx[peer], tgt[pick], (((1,), (1,)), ((), ())), preferred_element_type=jnp.float32
            ) * (2.0 * scale)
            for peer, pick in zip(peers, picks)
        ]
        turned = [jnp.transpose(grid) for grid in grids]
        rows = [logsum(b_col[pick] + grid_t) for pick, grid_t in zip(picks, turned)]
        for peer, row in zip(peers, rows):
            stats_out[0, peer] = row
        for d, peer in zip(offsets, peers):
            unless_zero(d, lambda peer=peer: stat_copy(0, peer, me).start())

        for peer, grid, grid_t in zip(peers, grids, turned):
            score[peer] = grid
            score_t[peer] = grid_t
        for peer in peers:
            keep_copy(peer).start()
            forward_copy(peer, side).start()

    spread(0, n // 4, arrivals)

    def finish_blocks(d):
        peer = lax.rem(me + d, n)
        id_copy(peer, me).wait_send()
        x_copy(peer, me).wait_send()

    def finish_forwards(q):
        keep_copy(q).wait()
        forward_copy(q, other).wait_recv()
        forward_copy(q, side).wait_send()

    for it in range(ITERS):
        if it == 1:
            loop(1, n, finish_blocks)
        if it == 2:
            loop(0, n, finish_forwards)
        if it > 0:
            stat_total(it - 1).wait_send()
            a_total(it - 1).wait_send()
            swap(it - 1).wait_send()
        stat_total(it).wait_recv()
        stats_in[it, me] = stats_out[it, me]

        def stat_row(p):
            stat_rows[pl.ds(p, 1), :] = stats_in[it, p]

        grouped(n, 8, stat_row)
        values, keys = stat_rows[...], source_keys[...]
        rows = [combine(values, keys, b) for b in range(blocks)]
        for b, row in enumerate(rows):
            rep_out[it, b:b + 1, :] = row
        swap(it).start()
        swap(it).wait_recv()
        top = jnp.maximum(rep_out[it], rep_in[it])
        total = jnp.exp(rep_out[it] - top) + jnp.exp(rep_in[it] - top)
        a_src[...] = -(top + jnp.log(total))

        def send_a(d):
            peer = lax.rem(me + far_first(d, n), n)
            a_send[it, peer] = a_src[pl.ds(jnp.maximum(source_pick[peer], 0), 1), :]
            a_copy(it, peer, me).start()

        spread(0, n - 1, send_a)
        a_in[it, me] = a_src[pl.ds(jnp.maximum(source_pick[me], 0), 1), :]

        a_total(it).wait_recv()

        def a_row(q):
            a_rows[pl.ds(q, 1), :] = a_in[it, q]

        grouped(n, 8, a_row)
        if it + 1 == ITERS:
            a_all[side] = a_rows[...]
            tail_copy(1, a_all, side).start()

        def column_visits(chunk):
            base = chunk * 16
            columns = columns_of(a_rows[pl.ds(pl.multiple_of(base, 16), 16), :])
            rows = [logsum(column + score[base + k]) for k, column in enumerate(columns)]
            for k, row in enumerate(rows):
                stat_rows[pl.ds(base + k, 1), :] = row

        loop(0, n // 16, column_visits)
        values, keys = stat_rows[...], id_keys[...]
        rows = [-combine(values, keys, b + first) for b in range(half)]
        for b, row in enumerate(rows):
            b_pad[b:b + 1, :] = row
        if it + 1 == ITERS:
            b_all[side] = b_pad[0:half, :]
        else:
            for b, column in enumerate(columns_of(b_pad[...])[:half]):
                b_col[first + b] = column

            def next_rows(group):
                offsets = [far_first(group * 8 + k, n) for k in range(8)]
                peers = [lax.rem(me + d, n) for d in offsets]
                rows = [logsum(b_col[local_id(q)] + score_t[q]) for q in peers]
                for q, row in zip(peers, rows):
                    stats_out[it + 1, q] = row
                for d, q in zip(offsets, peers):
                    unless_zero(d, lambda q=q: stat_copy(it + 1, q, me).start())

            spread(0, n // 8, next_rows)

    tail_copy(2, b_all, side).start()
    source_out[...] = EPSILON * (a_src[...] + x_sq[...])

    stat_total(ITERS - 1).wait_send()
    a_total(ITERS - 1).wait_send()
    swap(ITERS - 1).wait_send()
    for k, ref in enumerate((ids_all, a_all, b_all)):
        tail_copy(k, ref, other).wait_recv()
        tail_copy(k, ref, side).wait_send()
    ids_out[...] = ids_all[...]
    a_out[...] = a_all[...]
    for part in range(2):
        b_out[part * half:(part + 1) * half, :] = b_all[part]
    target_out[...] = EPSILON * (b_out[...] + y_sq[...])


def gradient_kernel(
    pairs, blocks, scale, ids, rx_hbm, a_rows, b_rows, tgt_hbm, source_in, target_in,
    out, source_out, target_out, rx, tgt, grad, b_col, mass, sems, out_sems,
):
    groups = pairs // 16

    def fetch(group):
        part = pl.ds(group * 16, 16)
        return pltpu.make_async_copy(rx_hbm.at[part], rx.at[part], sems.at[group])

    def store(b):
        return pltpu.make_async_copy(grad.at[b], out.at[b], out_sems.at[b])

    load_tgt = pltpu.make_async_copy(tgt_hbm, tgt, out_sems.at[blocks])
    load_tgt.start()
    loop(0, groups, lambda group: fetch(group).start())
    source_out[...] = source_in[...]
    target_out[...] = target_in[...]
    for b, column in enumerate(columns_of(b_rows[...])):
        b_col[b] = column

    def prepare(b):
        grad[b] = jnp.zeros(grad.shape[1:], jnp.float32)
        mass[b] = jnp.zeros((BLOCK, BLOCK), jnp.float32)

    grouped(blocks, 4, prepare)
    load_tgt.wait()

    def visit(group):
        fetch(group).wait()
        results = []
        for k in range(16):
            q = group * 16 + k
            target = ids[q, 0]
            pick = jnp.maximum(target, 0)
            grid = lax.dot_general(
                tgt[pick], rx[q], (((1,), (1,)), ((), ())), preferred_element_type=jnp.float32
            ) * (2.0 * scale)
            plan = jnp.exp(b_col[pick] + (grid + a_rows[pl.ds(q, 1), :]))
            plan = jnp.where(target >= 0, plan, 0.0)
            part = jnp.dot(plan.astype(jnp.bfloat16), rx[q], preferred_element_type=jnp.float32)
            results.append((pick, plan, part))
        for pick, plan, part in results:
            grad[pick] += part
            mass[pick] += plan

    loop(0, groups, visit)

    def finish(group):
        for k in range(4):
            b = group * 4 + k
            column = jnp.sum(mass[b], axis=1, keepdims=True)
            grad[b] = tgt[b].astype(jnp.float32) * column - grad[b]
        for k in range(4):
            store(group * 4 + k).start()

    loop(0, blocks // 4, finish)
    loop(0, blocks, lambda b: store(b).wait())


def on_device(src_points, tgt_points, pair_source, pair_target, pair_count):
    n = lax.axis_size("pts")
    reps = lax.axis_size("rep")
    rows, dim = src_points.shape
    blocks = rows // BLOCK
    half = blocks // reps
    scale = 1.0 / EPSILON / dim
    src = src_points.reshape(blocks, BLOCK, dim)
    tgt = tgt_points.reshape(blocks, BLOCK, dim)

    f32, bf16, i32 = jnp.float32, jnp.bfloat16, jnp.int32
    shape = jax.ShapeDtypeStruct
    vmem = pl.BlockSpec(memory_space=pltpu.VMEM)
    smem = pl.BlockSpec(memory_space=pltpu.SMEM)
    hbm = pl.BlockSpec(memory_space=pl.ANY)
    dma = pltpu.SemaphoreType.DMA
    with jax.named_scope("exchange_and_sweeps"):
        rx, ids, a_rows, b_rows, source_dual, target_dual = pl.pallas_call(
            functools.partial(exchange_kernel, n, blocks, half, scale),
            out_shape=(
                shape((reps, n, BLOCK, dim), bf16),
                shape((reps, n, BLOCK), i32),
                shape((reps, n, BLOCK), f32),
                shape((blocks, BLOCK), f32),
                shape((blocks, BLOCK), f32),
                shape((blocks, BLOCK), f32),
            ),
            in_specs=[smem, smem, smem, hbm, hbm],
            out_specs=(hbm, vmem, vmem, vmem, vmem, vmem),
            scratch_shapes=[
                pltpu.VMEM((blocks, BLOCK, dim), bf16),
                pltpu.VMEM((blocks, BLOCK, dim), bf16),
                pltpu.VMEM((n, BLOCK, dim), bf16),
                pltpu.VMEM((n, BLOCK, dim), bf16),
                pltpu.VMEM((n, BLOCK, BLOCK), f32),
                pltpu.VMEM((n, BLOCK, BLOCK), f32),
                pltpu.VMEM((blocks, BLOCK, BLOCK), f32),
                pltpu.VMEM((n, 1, BLOCK), i32),
                pltpu.VMEM((n, 1, BLOCK), i32),
                pltpu.VMEM((reps, n, BLOCK), i32),
                pltpu.SMEM((n, 1, BLOCK), i32),
                pltpu.VMEM((n, BLOCK), i32),
                pltpu.SMEM((n,), i32),
                pltpu.SMEM((n,), i32),
                pltpu.VMEM((n, BLOCK), i32),
                pltpu.VMEM((ITERS, n, 1, BLOCK), f32),
                pltpu.VMEM((ITERS, n, 1, BLOCK), f32),
                pltpu.VMEM((n, BLOCK), f32),
                pltpu.VMEM((ITERS, blocks, BLOCK), f32),
                pltpu.VMEM((ITERS, blocks, BLOCK), f32),
                pltpu.VMEM((blocks, BLOCK), f32),
                pltpu.VMEM((ITERS, n, 1, BLOCK), f32),
                pltpu.VMEM((ITERS, n, 1, BLOCK), f32),
                pltpu.VMEM((n, BLOCK), f32),
                pltpu.VMEM((reps, n, BLOCK), f32),
                pltpu.VMEM((reps, half, BLOCK), f32),
                pltpu.VMEM((-(-half // 8) * 8, BLOCK), f32),
                pltpu.VMEM((blocks, BLOCK), f32),
                pltpu.VMEM((blocks, BLOCK), f32),
                dma((3,)),
                dma((n,)), dma((n,)), dma((n,)), dma((n,)), dma((n,)), dma((n,)), dma((n,)),
                dma((ITERS,)), dma((ITERS,)), dma((ITERS,)), dma((ITERS,)),
                dma((ITERS,)), dma((ITERS,)), dma((3,)), dma((3,)),
            ],
            compiler_params=pltpu.CompilerParams(
                collective_id=0, has_side_effects=True, vmem_limit_bytes=VMEM_BYTES
            ),
            name="exchange_and_sweeps",
        )(pair_source, pair_target, pair_count, src, tgt)
    pairs = reps * n
    with jax.named_scope("gradient"):
        grad, source_dual, target_dual = pl.pallas_call(
            functools.partial(gradient_kernel, pairs, blocks, scale),
            out_shape=(
                shape((blocks, BLOCK, dim), f32),
                shape((blocks, BLOCK), f32),
                shape((blocks, BLOCK), f32),
            ),
            in_specs=[smem, hbm, vmem, vmem, hbm, vmem, vmem],
            out_specs=(hbm, vmem, vmem),
            scratch_shapes=[
                pltpu.VMEM((pairs, BLOCK, dim), bf16),
                pltpu.VMEM((blocks, BLOCK, dim), bf16),
                pltpu.VMEM((blocks, BLOCK, dim), f32),
                pltpu.VMEM((blocks, BLOCK, BLOCK), f32),
                pltpu.VMEM((blocks, BLOCK, BLOCK), f32),
                dma((pairs // 16,)),
                dma((blocks + 1,)),
            ],
            compiler_params=pltpu.CompilerParams(vmem_limit_bytes=VMEM_BYTES),
            name="gradient",
        )(
            ids.reshape(pairs, BLOCK),
            rx.reshape(pairs, BLOCK, dim),
            a_rows.reshape(pairs, BLOCK),
            b_rows,
            tgt,
            source_dual,
            target_dual,
        )
    return source_dual.reshape(-1), target_dual.reshape(-1), grad.reshape(rows, dim)


def solution(mesh):
    return jax.shard_map(
        on_device,
        mesh=mesh,
        in_specs=(
            P("pts", None),
            P("pts", None),
            P(("pts", "rep")),
            P(("pts", "rep")),
            P(("pts", "rep")),
        ),
        out_specs=(P("pts"), P("pts"), P("pts", None)),
        check_vma=False,
    )
```
